32 devices in a mesh: ctx: 16 (over z, y, core), tp: 2 (over x).
Axes of the slice: x: 2, y: 2, z: 4, core: 2. Of those that a mesh axis runs over, the one named last changes fastest.
Arguments:
- tokens: bfloat16 [6144, 3072], P('ctx', 'tp'), may hold values from -6 to 6
- queries: bfloat16 [6144, 2048], P('ctx', 'tp'), may hold values from -16 to 16
- key_rows: bfloat16 [6144, 2048], P('ctx', 'tp'), may hold values from -16 to 16
- value_rows: bfloat16 [6144, 2048], P('ctx', 'tp'), may hold values from -6 to 6
- clip_ids: int32 [6144], replicated, may hold values from 0 to 3, never falling along the last dimension, each value on 1 to 4608 neighbouring positions
- causal: int32 [4], replicated, may hold values 0 or 1
- modulation: float32 [3, 4, 3072], replicated, may hold values from -3 to 3
- w_mlp: bfloat16 [3072, 6144], P(None, 'tp'), may hold values from -0.109375 to 0.109375
- w_attn_out: bfloat16 [2048, 3072], P('tp'), may hold values from -1 to 1
- w_mlp_out: bfloat16 [6144, 3072], P('tp'), may hold values from -0.078125 to 0.078125
Outputs:
- mixed: float32 [6144, 3072], P(('ctx', 'tp'))
The draws below stay inside these ranges and needn't reach their ends.
Inputs may be any that keep to these rules, and one draw needn't show every extreme that they name: `clip_ids`: clip numbers never fall along the tokens; each of the 4 clips has 1 to 4608 tokens and one has exactly 4608.
All inputs are finite; a program needn't handle non-finite values.
Results may differ from the reference program's by a relative error of at most 0.0065.
Values may be sent and summed in bfloat16 or wider, within the bound.
No kernel may reach another device: no remote copies, remote signals or barrier semaphores. Data moves between devices by JAX's collectives and lax.ppermute only.
A program may use at most 192 MiB of HBM per device.

```python
import math
import jax
import jax.numpy as jnp
import numpy as np
from jax import lax

D = 3072
HEADS = 16
HD = 128
MLP = 6144
CLIPS = 4
TOKENS = 6144
MOST = 4608


def draw_queries(key, part):
    drawn_rows = jnp.clip(jax.random.normal(jax.random.fold_in(key, 1), (TOKENS, HEADS * HD), jnp.float32), -4.0, 4.0)
    return drawn_rows.astype(jnp.bfloat16)


def draw_key_rows(key, part):
    drawn_rows = jnp.clip(jax.random.normal(jax.random.fold_in(key, 2), (TOKENS, HEADS * HD), jnp.float32), -4.0, 4.0)
    return drawn_rows.astype(jnp.bfloat16)


def touch_ends(result, rng, low, largest):
    shape = result.shape
    index_at = [jax.random.randint(jax.random.fold_in(rng, axis), (), 0, shape[axis]) for axis in range(len(shape))]
    result = result.at[tuple(index_at)].set(low)
    longest = shape.index(max(shape))
    index_at[longest] = (index_at[longest] + 1) % shape[longest]
    return result.at[tuple(index_at)].set(largest)


def shard_levels(key, shape, shards, smallest, top_value):
    loudness = 1.0
    for axis_at, blocks in shards:
        steps = jax.random.uniform(jax.random.fold_in(jax.random.fold_in(key, 6), axis_at), (blocks,), jnp.float32, smallest / len(shards), top_value / len(shards))
        loudness = loudness * jnp.repeat(jnp.exp(steps), shape[axis_at] // blocks).reshape((-1,) + (1,) * (len(shape) - 1 - axis_at))
    return loudness


def split_up(amount, total, limit, lean):
    weights = [(1 << 20) // math.isqrt(standing ** lean) + 1 for standing in range(2, amount + 1)]
    surplus, counts = total - limit - (amount - 1), [1] * (amount - 1)
    while surplus > 0:
        candidates = [i for i in range(amount - 1) if counts[i] < limit]
        pool, budget = sum([weights[i] for i in candidates]), surplus
        for i in candidates:
            extra = min(limit - counts[i], max(1, budget * weights[i] // pool), surplus)
            counts[i] = counts[i] + extra
            surplus = surplus - extra
    return np.array([limit] + counts)


def uneven_parts(rng, amount, total, most, lean):
    if amount == 2:
        one = jax.random.randint(rng, (), max(1, total - most), min(most, total - 1) + 1)
        return jnp.stack([one, total - one])
    lengths = jnp.asarray(split_up(amount, total, most, lean), jnp.int32)
    pairs = (amount - 1) // 2
    donor, taker = lengths[1:1 + 2 * pairs:2], lengths[2:2 + 2 * pairs:2]
    slack = jnp.minimum(donor - 1, most - taker)
    passed = jax.random.randint(jax.random.fold_in(rng, 1), (pairs,), 0, 1 << 20) % (slack + 1)
    lengths = lengths.at[1:1 + 2 * pairs:2].set(donor - passed).at[2:2 + 2 * pairs:2].set(taker + passed)
    return lengths[jax.random.permutation(jax.random.fold_in(rng, 2), amount)]


def bell_draw(rng, shape, width, reach, shards=(), kind=jnp.bfloat16):
    result = jax.random.normal(rng, shape, jnp.float32) * width
    if len(shards) > 0:
        result = shard_levels(rng, shape, shards, -0.22, 0.18) * result
    return jnp.clip(result, min=-reach, max=reach).astype(kind)


def setup_inputs(seed: int = 0) -> dict:
    key_list = jax.random.split(jax.random.key(seed), 11)
    tokens = bell_draw(key_list[0], (TOKENS, D), 1.0, 6.0, ((0, 16), (1, 2)))
    queries = draw_queries(jax.random.fold_in(key_list[10], 71), 0)
    key_rows = draw_key_rows(jax.random.fold_in(key_list[10], 71), 0)
    value_rows = bell_draw(key_list[3], (TOKENS, HEADS * HD), 1.0, 6.0, ((0, 16), (1, 2)))
    clip_ids = jnp.searchsorted(jnp.cumsum(uneven_parts(key_list[4], CLIPS, TOKENS, MOST, 0)), jnp.arange(TOKENS), side="right").astype(jnp.int32)
    causal = touch_ends((jax.random.randint(key_list[5], (CLIPS,), 0, 2) < 1).astype(jnp.int32), jax.random.fold_in(key_list[5], 1), 0, 1)
    modulation = bell_draw(key_list[6], (3, CLIPS, D), 0.5, 3.0, (), jnp.float32)
    w_mlp = bell_draw(key_list[7], (D, MLP), D ** -0.5, 0.109375, ((1, 2),))
    w_attn_out = bell_draw(key_list[8], (HEADS * HD, D), (HEADS * HD // 64) ** -0.5, 1.0, ((0, 2),))
    w_mlp_out = bell_draw(key_list[9], (MLP, D), MLP ** -0.5, 0.078125, ((0, 2),))
    return {"tokens": tokens, "queries": queries, "key_rows": key_rows, "value_rows": value_rows, "clip_ids": clip_ids, "causal": causal, "modulation": modulation, "w_mlp": w_mlp, "w_attn_out": w_attn_out, "w_mlp_out": w_mlp_out}


neg_large = -1e+30
eps_norm = 1e-06

def attention(queries, key_rows, value_rows, clip_ids, causal):
    tile_width = math.gcd(TOKENS, 256)
    blocks = TOKENS // tile_width
    inverse_root = 1.0 / math.sqrt(HD)
    key_all = key_rows.astype(jnp.float32).reshape(TOKENS, HEADS, HD)
    value_all = value_rows.astype(jnp.float32).reshape(TOKENS, HEADS, HD)
    positions = jnp.arange(TOKENS, dtype=jnp.int32)
    causal_tok = causal[clip_ids]

    def one_block(tile_items):
        query_tile, pos_tile, id_tile, causal_tile = tile_items
        scores = jnp.einsum('ihd,jhd->hij', query_tile.astype(jnp.float32), key_all, precision=lax.Precision.HIGHEST) * inverse_root
        allowed = (id_tile[:, None] == clip_ids[None, :]) & ((causal_tile[:, None] == 0) | (positions[None, :] <= pos_tile[:, None]))
        scores = jnp.where(allowed[None], scores, neg_large)
        row_peak = lax.optimization_barrier(jnp.max(scores, axis=2, keepdims=True))
        weights = jnp.where(allowed[None], jnp.exp(scores - row_peak), 0.0).astype(jnp.bfloat16)
        weights = lax.optimization_barrier(weights).astype(jnp.float32)
        numerator = jnp.einsum('hij,jhd->ihd', weights, value_all, precision=lax.Precision.HIGHEST)
        denominator = jnp.transpose(lax.optimization_barrier(jnp.sum(weights, axis=2)))
        return (numerator / denominator[:, :, None]).astype(jnp.bfloat16).reshape(tile_width, HEADS * HD)
    attended_tiles = lax.map(one_block, (queries.reshape(blocks, tile_width, HEADS, HD), positions.reshape(blocks, tile_width), clip_ids.reshape(blocks, tile_width), causal_tok.reshape(blocks, tile_width)))
    return attended_tiles.reshape(TOKENS, HEADS * HD)

def reference(tokens, queries, key_rows, value_rows, clip_ids, causal, modulation, w_mlp, w_attn_out, w_mlp_out):
    token_values = tokens.astype(jnp.float32)
    row_mean = lax.optimization_barrier(jnp.mean(token_values, axis=1, keepdims=True))
    centred = token_values - row_mean
    row_var = lax.optimization_barrier(jnp.mean(centred * centred, axis=1, keepdims=True))
    normed = centred * lax.rsqrt(row_var + eps_norm)
    shift_rows = modulation[0][clip_ids]
    scale_rows = modulation[1][clip_ids]
    gate_rows = modulation[2][clip_ids]
    modulated = (normed * (1.0 + scale_rows) + shift_rows).astype(jnp.bfloat16)
    hidden = jax.nn.gelu(jnp.dot(modulated, w_mlp, preferred_element_type=jnp.float32), approximate=True).astype(jnp.bfloat16)
    attended = attention(queries, key_rows, value_rows, clip_ids, causal)
    branch = jnp.dot(attended, w_attn_out, preferred_element_type=jnp.float32) + jnp.dot(hidden, w_mlp_out, preferred_element_type=jnp.float32)
    return token_values + gate_rows * branch
```

```python
import functools
import math

import jax
import jax.numpy as jnp
from jax import lax
from jax.experimental import pallas as pl
from jax.experimental.pallas import tpu as pltpu
from jax.sharding import PartitionSpec as P

HD = 128
LANES = 128
ONES_ROWS = 8
MASKED = -3e38
START_MAX = -1e30
EPS_NORM = 1e-06
EXP2_SCALE = math.log2(math.e) / math.sqrt(HD)
VMEM_LIMIT = 48 << 20

ANY = pl.BlockSpec(memory_space=pl.ANY)
SMEM = pl.BlockSpec(memory_space=pltpu.SMEM)
VMEM = pl.BlockSpec(memory_space=pltpu.VMEM)


def params():
    return pltpu.CompilerParams(vmem_limit_bytes=VMEM_LIMIT)


def cost(flops, nbytes, exps=0):
    return pl.CostEstimate(flops=flops, bytes_accessed=nbytes, transcendentals=exps)


def split_kernel(chips, chip_ref, q_ref, k_ref, v_ref, *outs):
    rows = q_ref.shape[0]
    for k in range(chips):
        head = lax.bitwise_xor(chip_ref[0], k)
        columns = pl.ds(pl.multiple_of(head * HD, HD), HD)
        kv_out, q_out = outs[2 * k], outs[2 * k + 1]
        q_out[...] = q_ref[:, columns]
        kv_out[0] = k_ref[:, columns]
        for at in range(0, rows, LANES):
            block = v_ref[at : at + LANES, columns].astype(jnp.float32)
            kv_out[1, at : at + LANES, :] = jnp.transpose(block).astype(jnp.bfloat16)


def split_heads(chip, chips, queries, key_rows, value_rows):
    rows = queries.shape[0]
    shapes = []
    for _ in range(chips):
        shapes.append(jax.ShapeDtypeStruct((2, rows, HD), jnp.bfloat16))
        shapes.append(jax.ShapeDtypeStruct((rows, HD), jnp.bfloat16))
    outs = pl.pallas_call(
        functools.partial(split_kernel, chips),
        out_shape=shapes,
        in_specs=[SMEM, VMEM, VMEM, VMEM],
        out_specs=[VMEM] * len(shapes),
        compiler_params=params(),
        name="split_heads",
    )(chip[None], queries, key_rows, value_rows)
    return outs[0::2], outs[1::2]


def span_of(scalars, clips, pos):
    low = jnp.zeros_like(pos)
    high = jnp.zeros_like(pos)
    for clip in range(clips):
        inside = pos >= scalars[clip]
        end = jnp.where(scalars[clips + 1 + clip] != 0, pos + 1, scalars[clip + 1])
        low = jnp.where(inside, scalars[clip], low)
        high = jnp.where(inside, end, high)
    return low, high


def attention_kernel(clips, n_query, n_kv, key_tile, scalars, *refs):
    query_hbm = refs[:n_query]
    kv_hbm = refs[n_query : n_query + n_kv]
    out_hbm = refs[n_query + n_kv : 2 * n_query + n_kv]
    q, k, v, out, total, peak, score_a, score_b, block_peak, sems = refs[2 * n_query + n_kv :]
    rows = q.shape[1]
    all_keys = k.shape[0]
    query_at = 2 * clips + 1
    kv_at = query_at + n_query
    copies = []
    for i in range(n_query):
        copies.append(pltpu.make_async_copy(query_hbm[i], q.at[i], sems.at[len(copies)]))
    for i in range(n_kv):
        count = kv_hbm[i].shape[1]
        base = pl.multiple_of(scalars[kv_at + i], LANES)
        copies.append(
            pltpu.make_async_copy(kv_hbm[i].at[0], k.at[pl.ds(base, count)], sems.at[len(copies)])
        )
        for at in range(0, count, LANES):
            copies.append(
                pltpu.make_async_copy(
                    kv_hbm[i].at[1, at : at + LANES],
                    v.at[0:HD, pl.ds(pl.multiple_of(base + at, LANES), LANES)],
                    sems.at[len(copies)],
                )
            )
    for copy in copies:
        copy.start()
    v[HD:, :] = jnp.ones((ONES_ROWS, all_keys), jnp.bfloat16)
    for copy in copies:
        copy.wait()
    scores = [score_a, score_b]

    def one_piece(piece, _):
        base = scalars[query_at + piece]
        low_first, high_first = span_of(scalars, clips, base)
        low_last, high_last = span_of(scalars, clips, base + rows - 1)
        begin = low_first // key_tile
        end = (high_last + key_tile - 1) // key_tile
        full_from = (low_last + key_tile - 1) // key_tile
        full_to = high_first // key_tile
        pos = base + lax.broadcasted_iota(jnp.int32, (1, rows), 1)
        low, high = span_of(scalars, clips, pos)
        total[...] = jnp.zeros_like(total)
        peak[...] = jnp.full_like(peak, START_MAX)

        def multiply(tile, slot):
            keys = k[pl.ds(pl.multiple_of(tile * key_tile, key_tile), key_tile), :]
            block = lax.dot_general(
                keys, q[piece], (((1,), (1,)), ((), ())), preferred_element_type=jnp.float32
            )
            scores[slot][...] = block
            block_peak[slot] = jnp.max(block, axis=0, keepdims=True)

        def mask(tile, slot):
            @pl.when((tile < full_from) | (tile >= full_to))
            def _():
                key_pos = tile * key_tile + lax.broadcasted_iota(jnp.int32, (key_tile, 1), 0)
                allowed = (key_pos >= low) & (key_pos < high)
                block = jnp.where(allowed, scores[slot][...], MASKED)
                scores[slot][...] = block
                block_peak[slot] = jnp.max(block, axis=0, keepdims=True)

        def gather(tile, slot):
            old = peak[...]
            new = jnp.maximum(old, block_peak[slot])
            peak[...] = new
            factor = jnp.exp2((old - new) * EXP2_SCALE)
            weights = jnp.exp2(scores[slot][...] * EXP2_SCALE - new * EXP2_SCALE)
            values = v[:, pl.ds(pl.multiple_of(tile * key_tile, key_tile), key_tile)]
            total[...] = total[...] * factor + jnp.dot(
                values, weights.astype(jnp.bfloat16), preferred_element_type=jnp.float32
            )

        multiply(begin, 0)
        mask(begin, 0)
        count = end - begin

        def two_tiles(pair, _):
            tile = begin + 2 * pair
            multiply(tile + 1, 1)
            gather(tile, 0)
            mask(tile + 1, 1)
            later = jnp.minimum(tile + 2, end - 1)
            multiply(later, 0)
            gather(tile + 1, 1)
            mask(later, 0)
            return 0

        lax.fori_loop(0, count // 2, two_tiles, 0)

        @pl.when(count % 2 == 1)
        def _():
            gather(end - 1, 0)

        both = total[...]
        out[piece] = jnp.transpose(both[:HD] / both[HD : HD + 1]).astype(jnp.bfloat16)
        return 0

    lax.fori_loop(0, n_query, one_piece, 0)
    copies = [
        pltpu.make_async_copy(out.at[i], out_hbm[i], sems.at[i]) for i in range(n_query)
    ]
    for copy in copies:
        copy.start()
    for copy in copies:
        copy.wait()


def attention(clips, scalars, query_pieces, kv_pieces):
    rows = query_pieces[0].shape[0]
    n_query, n_kv = len(query_pieces), len(kv_pieces)
    all_keys = sum(piece.shape[1] for piece in kv_pieces)
    key_tile = math.gcd(all_keys, 768)
    n_sems = n_query + sum(1 + piece.shape[1] // LANES for piece in kv_pieces)
    return pl.pallas_call(
        functools.partial(attention_kernel, clips, n_query, n_kv, key_tile),
        out_shape=[jax.ShapeDtypeStruct((rows, HD), jnp.bfloat16)] * n_query,
        in_specs=[SMEM] + [ANY] * (n_query + n_kv),
        out_specs=[ANY] * n_query,
        scratch_shapes=[
            pltpu.VMEM((n_query, rows, HD), jnp.bfloat16),
            pltpu.VMEM((all_keys, HD), jnp.bfloat16),
            pltpu.VMEM((HD + ONES_ROWS, all_keys), jnp.bfloat16),
            pltpu.VMEM((n_query, rows, HD), jnp.bfloat16),
            pltpu.VMEM((HD + ONES_ROWS, rows), jnp.float32),
            pltpu.VMEM((1, rows), jnp.float32),
            pltpu.VMEM((key_tile, rows), jnp.float32),
            pltpu.VMEM((key_tile, rows), jnp.float32),
            pltpu.VMEM((2, 1, rows), jnp.float32),
            pltpu.SemaphoreType.DMA((n_sems,)),
        ],
        compiler_params=params(),
        cost_estimate=cost(
            4 * n_query * rows * all_keys * HD, 4 * all_keys * HD, n_query * rows * all_keys
        ),
        name="attention",
    )(scalars, *query_pieces, *kv_pieces)


def value_blocks(values):
    count = values.shape[0]
    return jnp.swapaxes(values.reshape(count // LANES, LANES, HD), 1, 2).reshape(count, HD)


def select_rows(ids, table, clips):
    picked = jnp.broadcast_to(table[0:1], (ids.shape[0], table.shape[1]))
    for clip in range(1, clips):
        picked = jnp.where(ids == clip, table[clip : clip + 1], picked)
    return picked


def mlp_kernel(clips, n_parts, scalars, ids_ref, modulation_ref, *refs):
    parts = refs[:n_parts]
    w_in, w_out, branch, modulated = refs[n_parts:]
    step = pl.program_id(0)
    rows, width = modulated.shape

    @pl.when(step == 0)
    def _():
        part_width = width // n_parts
        mean = sum(
            jnp.sum(part[...].astype(jnp.float32), axis=1, keepdims=True) for part in parts
        ) / width
        variance = sum(
            jnp.sum((part[...].astype(jnp.float32) - mean) ** 2, axis=1, keepdims=True)
            for part in parts
        ) / width
        inverse = lax.rsqrt(variance + EPS_NORM)
        ids = ids_ref[...]
        for i, part in enumerate(parts):
            columns = pl.ds(pl.multiple_of(scalars[i] * part_width, LANES), part_width)
            normed = (part[...].astype(jnp.float32) - mean) * inverse
            shift = select_rows(ids, modulation_ref[0, :, columns], clips)
            scale = select_rows(ids, modulation_ref[1, :, columns], clips)
            modulated[:, columns] = (normed * (1.0 + scale) + shift).astype(jnp.bfloat16)

    hidden = jax.nn.gelu(
        jnp.dot(modulated[...], w_in[...], preferred_element_type=jnp.float32), approximate=True
    ).astype(jnp.bfloat16)
    product = jnp.dot(hidden, w_out[...], preferred_element_type=jnp.float32)

    @pl.when(step == 0)
    def _():
        branch[...] = product

    @pl.when(step > 0)
    def _():
        branch[...] += product


def mlp(clips, order, ids, modulation, parts, w_in, w_out):
    rows = parts[0].shape[0]
    width, units = w_in.shape
    block = math.gcd(units, 512)
    return pl.pallas_call(
        functools.partial(mlp_kernel, clips, len(parts)),
        grid=(units // block,),
        out_shape=jax.ShapeDtypeStruct((rows, width), jnp.float32),
        in_specs=[SMEM, VMEM, VMEM]
        + [VMEM] * len(parts)
        + [
            pl.BlockSpec((width, block), lambda i: (0, i)),
            pl.BlockSpec((block, width), lambda i: (i, 0)),
        ],
        out_specs=pl.BlockSpec((rows, width), lambda i: (0, 0)),
        scratch_shapes=[pltpu.VMEM((rows, width), jnp.bfloat16)],
        compiler_params=params(),
        cost_estimate=cost(4 * rows * width * units, 4 * width * units + 4 * rows * width),
        name="mlp",
    )(order, ids[:, None], modulation, *parts, w_in, w_out)


def project_kernel(heads, scalars, *refs):
    attended = refs[:heads]
    w_ref, mlp_ref, kept, sent, gathered = refs[heads:]
    share = kept.shape[0]
    for i in range(heads):
        gathered[:, pl.ds(pl.multiple_of(scalars[i] * HD, HD), HD)] = attended[i][...]
    mine = pl.ds(pl.multiple_of(scalars[heads] * share, share), share)
    other = pl.ds(pl.multiple_of(scalars[heads + 1] * share, share), share)
    kept[...] = mlp_ref[mine, :] + jnp.dot(
        gathered[mine, :], w_ref[...], preferred_element_type=jnp.float32
    )
    sent[...] = (
        mlp_ref[other, :]
        + jnp.dot(gathered[other, :], w_ref[...], preferred_element_type=jnp.float32)
    ).astype(jnp.bfloat16)


def project(scalars, attended, w_attn_out, mlp_branch):
    rows, width = mlp_branch.shape
    heads = len(attended)
    inputs = w_attn_out.shape[0]
    block = math.gcd(width, 1024)
    return pl.pallas_call(
        functools.partial(project_kernel, heads),
        grid=(width // block,),
        out_shape=[
            jax.ShapeDtypeStruct((rows // 2, width), jnp.float32),
            jax.ShapeDtypeStruct((rows // 2, width), jnp.bfloat16),
        ],
        in_specs=[SMEM]
        + [VMEM] * heads
        + [
            pl.BlockSpec((inputs, block), lambda i: (0, i)),
            pl.BlockSpec((rows, block), lambda i: (0, i)),
        ],
        out_specs=[
            pl.BlockSpec((rows // 2, block), lambda i: (0, i)),
            pl.BlockSpec((rows // 2, block), lambda i: (0, i)),
        ],
        scratch_shapes=[pltpu.VMEM((rows, inputs), jnp.bfloat16)],
        compiler_params=params(),
        cost_estimate=cost(2 * rows * width * inputs, 2 * width * inputs + 4 * rows * width),
        name="project",
    )(scalars, *attended, w_attn_out, mlp_branch)


def per_device(
    tokens,
    queries,
    key_rows,
    value_rows,
    clip_ids,
    causal,
    modulation,
    w_mlp,
    w_attn_out,
    w_mlp_out,
):
    local_rows = queries.shape[0]
    heads = queries.shape[1] // HD
    clips = causal.shape[0]
    tp_size = lax.axis_size("tp")
    ctx_size = lax.axis_size("ctx")
    here = lax.axis_index("ctx")
    tp_here = lax.axis_index("tp")
    first_row = here * local_rows
    own_ids = lax.dynamic_slice_in_dim(clip_ids, first_row, local_rows)
    clip_starts = jnp.sum(
        (clip_ids[None, :] < jnp.arange(clips + 1, dtype=jnp.int32)[:, None]).astype(jnp.int32),
        axis=1,
    )
    clip_scalars = jnp.concatenate([clip_starts, causal])
    chips = ctx_size // 2
    exchange = ctx_size % 2 == 0 and heads == chips and chips & (chips - 1) == 0
    pair = tp_size == 2

    if pair:
        other_half = lax.ppermute(tokens, "tp", [(0, 1), (1, 0)])
        parts = [tokens, other_half]
        order = jnp.stack([tp_here, 1 - tp_here])
    else:
        parts = [lax.all_gather(tokens, "tp", axis=1, tiled=True)]
        order = jnp.zeros((1,), jnp.int32)

    if exchange:
        chip, core = here // 2, here % 2
        peers = [lax.bitwise_xor(chip, k) for k in range(chips)]

        def to_chip(array, k):
            if k == 0:
                return array
            return lax.ppermute(
                array, "ctx", [(2 * i + c, 2 * (i ^ k) + c) for i in range(chips) for c in (0, 1)]
            )

        kv_sent, query_sent = split_heads(chip, chips, queries, key_rows, value_rows)
        kv_own = [to_chip(piece, k) for k, piece in enumerate(kv_sent)]
        query_pieces = [to_chip(piece, k) for k, piece in enumerate(query_sent)]
        swap = [(2 * i + c, 2 * i + 1 - c) for i in range(chips) for c in (0, 1)]
        kv_pieces = list(kv_own)
        for piece in kv_own:
            kv_pieces.append(lax.ppermute(piece, "ctx", swap))
        rows_at = [peer * (2 * local_rows) + core * local_rows for peer in peers]
        others_at = [peer * (2 * local_rows) + (1 - core) * local_rows for peer in peers]
        scalars = jnp.concatenate([clip_scalars, jnp.stack(rows_at + rows_at + others_at)])
    mlp_branch = mlp(clips, order, own_ids, modulation, parts, w_mlp, w_mlp_out)
    if exchange:
        outs = attention(clips, scalars, query_pieces, kv_pieces)
        attended = [to_chip(piece, k) for k, piece in enumerate(outs)]
        head_order = jnp.stack(peers)
    else:
        all_keys = lax.all_gather(key_rows, "ctx", axis=0, tiled=True)
        all_values = lax.all_gather(value_rows, "ctx", axis=0, tiled=True)
        scalars = jnp.concatenate([clip_scalars, jnp.stack([first_row, 0])])
        attended = []
        for head in range(heads):
            columns = slice(head * HD, (head + 1) * HD)
            kv = jnp.stack([all_keys[:, columns], value_blocks(all_values[:, columns])])
            attended.extend(attention(clips, scalars, [queries[:, columns]], [kv]))
        head_order = jnp.arange(heads, dtype=jnp.int32)

    share = local_rows // tp_size
    if pair:
        kept, sent = project(
            jnp.concatenate([head_order, order]), attended, w_attn_out, mlp_branch
        )
        arrived = lax.ppermute(sent, "tp", [(0, 1), (1, 0)])
        branch = kept + arrived.astype(jnp.float32)
    else:
        branch = lax.psum_scatter(
            mlp_branch
            + jnp.dot(
                jnp.concatenate(attended, axis=1), w_attn_out, preferred_element_type=jnp.float32
            ),
            "tp",
            scatter_dimension=0,
            tiled=True,
        )
    first_share = tp_here * share
    own = [lax.dynamic_slice_in_dim(part, first_share, share, 0) for part in parts]
    if pair:
        residual = jnp.where(
            tp_here == 0, jnp.concatenate(own, axis=1), jnp.concatenate(own[::-1], axis=1)
        )
    else:
        residual = own[0]
    share_ids = lax.dynamic_slice_in_dim(own_ids, first_share, share)
    gate_rows = select_rows(share_ids[:, None], modulation[2], clips)
    return residual.astype(jnp.float32) + gate_rows * branch


def solution(mesh):
    in_specs = (
        P("ctx", "tp"),
        P("ctx", "tp"),
        P("ctx", "tp"),
        P("ctx", "tp"),
        P(),
        P(),
        P(),
        P(None, "tp"),
        P("tp", None),
        P("tp", None),
    )
    out_specs = P(("ctx", "tp"), None)
    return jax.shard_map(
        per_device, mesh=mesh, in_specs=in_specs, out_specs=out_specs, check_vma=False
    )
```

```python
import functools
import math

import jax
import jax.numpy as jnp
from jax import lax
from jax.experimental import pallas as pl
from jax.experimental.pallas import tpu as pltpu
from jax.sharding import PartitionSpec as P

HD = 128
LANES = 128
ONES_ROWS = 8
KEY_WIDTH = 2 * HD
MASKED = -3e38
COST_SCALE = 1
SPLIT_GRANT = 62
MLP_GRANT = 44
PROJECT_GRANT = 48
START_MAX = -1e30
EPS_NORM = 1e-06
EXP2_SCALE = math.log2(math.e) / math.sqrt(HD)

ANY = pl.BlockSpec(memory_space=pl.ANY)
HBM = pl.BlockSpec(memory_space=pltpu.HBM)
SMEM = pl.BlockSpec(memory_space=pltpu.SMEM)
VMEM = pl.BlockSpec(memory_space=pltpu.VMEM)


def params(mebibytes):
    return pltpu.CompilerParams(vmem_limit_bytes=mebibytes << 20)


def cost(flops, nbytes, exps=0):
    return pl.CostEstimate(
        flops=flops // COST_SCALE, bytes_accessed=nbytes // COST_SCALE, transcendentals=exps // COST_SCALE
    )


def split_kernel(
    ways, chunk_rows, scalars, q_hbm, k_hbm, v_hbm, keep_hbm, give_hbm, q, k, v, keep, give, sems
):
    rows = q.shape[0]
    share = rows // 2
    copies = [
        pltpu.make_async_copy(source, target, sems.at[i])
        for i, (source, target) in enumerate(((k_hbm, k), (v_hbm, v), (q_hbm, q)))
    ]
    for copy in copies:
        copy.start()
    for copy in copies:
        copy.wait()
    for side, out in enumerate((give, keep)):
        for m in range(ways):
            head = scalars[side * ways + m]
            columns = pl.ds(pl.multiple_of(head * HD, HD), HD)
            out[m, 0] = k[:, columns]
            for at in range(0, rows, LANES):
                block = v[at : at + LANES, columns].astype(jnp.float32)
                out[m, 1, at : at + LANES, :] = jnp.transpose(block).astype(jnp.bfloat16)
            first = 0
            for count in chunk_rows:
                half = count // 2
                start = 2 * first
                out[m, 2, start : start + half] = q[first : first + half, columns]
                out[m, 2, start + half : start + count] = q[
                    share + first : share + first + half, columns
                ]
                first += half
        copies.append(
            pltpu.make_async_copy(out, (give_hbm, keep_hbm)[side], sems.at[len(copies)])
        )
        copies[-1].start()
    copies[-2].wait()
    copies[-1].wait()


def split_heads(scalars, ways, chunk_rows, queries, key_rows, value_rows):
    rows = queries.shape[0]
    shape = jax.ShapeDtypeStruct((ways, 3, rows, HD), jnp.bfloat16)
    return pl.pallas_call(
        functools.partial(split_kernel, ways, chunk_rows),
        out_shape=[shape, shape],
        in_specs=[SMEM, HBM, HBM, HBM],
        out_specs=[ANY, ANY],
        scratch_shapes=[pltpu.VMEM(queries.shape, jnp.bfloat16)] * 3
        + [pltpu.VMEM(shape.shape, jnp.bfloat16)] * 2
        + [pltpu.SemaphoreType.DMA((5,))],
        compiler_params=params(SPLIT_GRANT),
        name="split_heads",
    )(scalars, queries, key_rows, value_rows)


def pack_kernel(ways, keep, got, *refs):
    outs, sems = refs[:ways], refs[ways]
    copies = []
    for m in reversed(range(ways)):
        for i, source in enumerate((keep, got)):
            copies.append(
                pltpu.make_async_copy(source.at[m], outs[m].at[:, i], sems.at[2 * m + i])
            )
            copies[-1].start()
    for copy in copies:
        copy.wait()


def pack(keep, got):
    ways, arrays, rows, _ = keep.shape
    return pl.pallas_call(
        functools.partial(pack_kernel, ways),
        out_shape=[jax.ShapeDtypeStruct((arrays, 2, rows, HD), jnp.bfloat16)] * ways,
        in_specs=[ANY, ANY],
        out_specs=[ANY] * ways,
        scratch_shapes=[pltpu.SemaphoreType.DMA((2 * ways,))],
        compiler_params=params(4),
        name="pack",
    )(keep, got)


def clip_lanes(scalars, clips):
    lane = lax.broadcasted_iota(jnp.int32, (1, HD), 1)
    low = jnp.zeros_like(lane)
    high = jnp.zeros_like(lane)
    for clip in range(clips):
        low = jnp.where(lane == clip, scalars[clip], low)
        high = jnp.where(lane == clip, scalars[clip + 1], high)
    return low, high


def assemble_kernel(clips, n_kv, scalars, *refs):
    pieces = refs[:n_kv]
    k, v, sems = refs[n_kv:]
    all_keys = k.shape[0]
    copies = []

    def load(source, target):
        copies.append(pltpu.make_async_copy(source, target, sems.at[len(copies)]))
        copies[-1].start()

    at_scalar = 2 * clips + 1
    for piece in pieces:
        groups, count = piece.shape[1:3]
        for group in range(groups):
            base = pl.multiple_of(scalars[at_scalar], LANES)
            at_scalar += 1
            load(piece.at[0, group], k.at[pl.ds(base, count), 0:HD])
            for at in range(0, count, LANES):
                columns = pl.ds(pl.multiple_of(base + at, LANES), LANES)
                load(piece.at[1, group, at : at + LANES], v.at[0:HD, columns])
    low, high = clip_lanes(scalars, clips)
    step = math.gcd(all_keys, 768)
    for at in range(0, all_keys, step):
        pos = at + lax.broadcasted_iota(jnp.int32, (step, HD), 0)
        inside = (pos >= low) & (pos < high)
        k[at : at + step, HD:] = jnp.where(inside, 1.0, 0.0).astype(jnp.bfloat16)
    v[HD:, :] = jnp.ones((v.shape[0] - HD, all_keys), jnp.bfloat16)
    for copy in copies:
        copy.wait()


def assemble(clips, scalars, kv_pieces):
    all_keys = sum(piece.shape[1] * piece.shape[2] for piece in kv_pieces)
    n_sems = sum(piece.shape[1] * (1 + piece.shape[2] // LANES) for piece in kv_pieces)
    return pl.pallas_call(
        functools.partial(assemble_kernel, clips, len(kv_pieces)),
        out_shape=[
            jax.ShapeDtypeStruct((all_keys, KEY_WIDTH), jnp.bfloat16),
            jax.ShapeDtypeStruct((HD + ONES_ROWS, all_keys), jnp.bfloat16),
        ],
        in_specs=[SMEM] + [ANY] * len(kv_pieces),
        out_specs=[VMEM, VMEM],
        scratch_shapes=[pltpu.SemaphoreType.DMA((n_sems,))],
        compiler_params=params(16),
        name="assemble",
    )(scalars, *kv_pieces)


def span_of(scalars, clips, pos):
    low = jnp.zeros_like(pos)
    high = jnp.zeros_like(pos)
    for clip in range(clips):
        inside = pos >= scalars[clip]
        end = jnp.where(scalars[clips + 1 + clip] != 0, pos + 1, scalars[clip + 1])
        low = jnp.where(inside, scalars[clip], low)
        high = jnp.where(inside, end, high)
    return low, high


def attention_kernel(clips, share, start, key_tile, scalars, k, v, *refs):
    n_query = (len(refs) - 8) // 2
    query_hbm = refs[:n_query]
    out_hbm = refs[n_query : 2 * n_query]
    q, out, total, peak, score_a, score_b, block_peak, sems = refs[2 * n_query :]
    width = q.shape[1]
    groups, rows, _ = out_hbm[0].shape
    half = rows // 2
    query_at = 2 * clips + 1
    none_causal = 1 << 30
    copies = []
    for i in range(n_query):
        arrays = query_hbm[i].shape[0]
        for group in range(groups):
            copies.append(
                pltpu.make_async_copy(
                    query_hbm[i].at[arrays - 1, group, start : start + rows],
                    q.at[i, group * rows : (group + 1) * rows, 0:HD],
                    sems.at[i * groups + group],
                )
            )
            copies[-1].start()
    clip_low, clip_high = clip_lanes(scalars, clips)
    for copy in copies:
        copy.wait()
    scores = [score_a, score_b]

    def positions(shape, axis, firsts):
        index = lax.broadcasted_iota(jnp.int32, shape, axis)
        pos = index
        for group, first in enumerate(firsts):
            at = group * rows
            pos = jnp.where(index >= at, index + (first - at), pos)
            pos = jnp.where(index >= at + half, index + (first + share - at - half), pos)
        return pos

    def one_tile(piece, _):
        firsts = [scalars[query_at + piece * groups + group] for group in range(groups)]
        begin, end, causal_from = none_causal, 0, none_causal
        for first in firsts:
            last = first + share + half - 1
            begin = jnp.minimum(begin, span_of(scalars, clips, first)[0])
            end = jnp.maximum(end, span_of(scalars, clips, last)[1])
            for clip in range(clips):
                met = (first < scalars[clip + 1]) & (last >= scalars[clip])
                met = met & (scalars[clips + 1 + clip] != 0)
                causal_from = jnp.where(
                    met, jnp.minimum(causal_from, jnp.maximum(first, scalars[clip])), causal_from
                )
        begin = begin // key_tile
        end = (end + key_tile - 1) // key_tile
        pos = positions((1, width), 1, firsts)
        last_key = jnp.full_like(pos, none_causal)
        for clip in range(clips):
            inside = (pos >= scalars[clip]) & (pos < scalars[clip + 1])
            inside = inside & (scalars[clips + 1 + clip] != 0)
            last_key = jnp.where(inside, pos, last_key)
        row_pos = positions((width, HD), 0, firsts)
        inside = (row_pos >= clip_low) & (row_pos < clip_high)
        q[piece, :, HD:] = jnp.where(inside, 0.0, MASKED).astype(jnp.bfloat16)
        total[...] = jnp.zeros_like(total)
        peak[...] = jnp.full_like(peak, START_MAX)

        def multiply(tile, slot):
            keys = k[pl.ds(pl.multiple_of(tile * key_tile, key_tile), key_tile), :]
            block = lax.dot_general(
                keys, q[piece], (((1,), (1,)), ((), ())), preferred_element_type=jnp.float32
            )
            scores[slot][...] = block
            block_peak[slot] = jnp.max(block, axis=0, keepdims=True)

        def mask(tile, slot):
            @pl.when((tile + 1) * key_tile - 1 > causal_from)
            def _():
                key_pos = tile * key_tile + lax.broadcasted_iota(jnp.int32, (key_tile, 1), 0)
                block = jnp.where(key_pos <= last_key, scores[slot][...], MASKED)
                scores[slot][...] = block
                block_peak[slot] = jnp.max(block, axis=0, keepdims=True)

        def gather(tile, slot):
            old = peak[...]
            new = jnp.maximum(old, block_peak[slot])
            peak[...] = new
            factor = jnp.exp2((old - new) * EXP2_SCALE)
            weights = jnp.exp2(scores[slot][...] * EXP2_SCALE - new * EXP2_SCALE)
            values = v[:, pl.ds(pl.multiple_of(tile * key_tile, key_tile), key_tile)]
            total[...] = total[...] * factor + jnp.dot(
                values, weights.astype(jnp.bfloat16), preferred_element_type=jnp.float32
            )

        multiply(begin, 0)
        mask(begin, 0)
        count = end - begin

        def two_tiles(pair, _):
            tile = begin + 2 * pair
            multiply(tile + 1, 1)
            gather(tile, 0)
            mask(tile + 1, 1)
            later = jnp.minimum(tile + 2, end - 1)
            multiply(later, 0)
            gather(tile + 1, 1)
            mask(later, 0)
            return 0

        lax.fori_loop(0, count // 2, two_tiles, 0)

        @pl.when(count % 2 == 1)
        def _():
            gather(end - 1, 0)

        both = total[...]
        out[piece] = jnp.transpose(both[:HD] / both[HD : HD + 1]).astype(jnp.bfloat16)
        return 0

    lax.fori_loop(0, n_query, one_tile, 0)
    copies = []
    for i in range(n_query):
        for group in range(groups):
            copies.append(
                pltpu.make_async_copy(
                    out.at[i, group * rows : (group + 1) * rows],
                    out_hbm[i].at[group],
                    sems.at[i * groups + group],
                )
            )
            copies[-1].start()
    for copy in copies:
        copy.wait()


def attention(clips, scalars, queries, start, rows, k, v, share, name):
    n_query = len(queries)
    groups = queries[0].shape[1]
    width = groups * rows
    all_keys = k.shape[0]
    key_tile = math.gcd(all_keys, 768)
    return pl.pallas_call(
        functools.partial(attention_kernel, clips, share, start, key_tile),
        out_shape=[jax.ShapeDtypeStruct((groups, rows, HD), jnp.bfloat16)] * n_query,
        in_specs=[SMEM, VMEM, VMEM] + [ANY] * n_query,
        out_specs=[ANY] * n_query,
        scratch_shapes=[
            pltpu.VMEM((n_query, width, KEY_WIDTH), jnp.bfloat16),
            pltpu.VMEM((n_query, width, HD), jnp.bfloat16),
            pltpu.VMEM((HD + ONES_ROWS, width), jnp.float32),
            pltpu.VMEM((1, width), jnp.float32),
            pltpu.VMEM((key_tile, width), jnp.float32),
            pltpu.VMEM((key_tile, width), jnp.float32),
            pltpu.VMEM((2, 1, width), jnp.float32),
            pltpu.SemaphoreType.DMA((n_query * groups,)),
        ],
        compiler_params=params(20),
        cost_estimate=cost(
            4 * n_query * width * all_keys * HD, 4 * all_keys * HD, n_query * width * all_keys
        ),
        name=name,
    )(scalars, k, v, *queries)


def value_blocks(values):
    count = values.shape[0]
    return jnp.swapaxes(values.reshape(count // LANES, LANES, HD), 1, 2).reshape(count, HD)


def select_rows(ids, table, clips):
    picked = jnp.broadcast_to(table[0:1], (ids.shape[0], table.shape[1]))
    for clip in range(1, clips):
        picked = jnp.where(ids == clip, table[clip : clip + 1], picked)
    return picked


def mlp_in_kernel(clips, n_parts, scalars, ids_ref, modulation_ref, *refs):
    parts = refs[:n_parts]
    w_in, hidden, modulated = refs[n_parts:]
    width = modulated.shape[1]

    @pl.when(pl.program_id(0) == 0)
    def _():
        part_width = width // n_parts
        mean = sum(
            jnp.sum(part[...].astype(jnp.float32), axis=1, keepdims=True) for part in parts
        ) / width
        variance = sum(
            jnp.sum((part[...].astype(jnp.float32) - mean) ** 2, axis=1, keepdims=True)
            for part in parts
        ) / width
        inverse = lax.rsqrt(variance + EPS_NORM)
        ids = ids_ref[...]
        for i, part in enumerate(parts):
            columns = pl.ds(pl.multiple_of(scalars[i] * part_width, LANES), part_width)
            normed = (part[...].astype(jnp.float32) - mean) * inverse
            shift = select_rows(ids, modulation_ref[0, :, columns], clips)
            scale = select_rows(ids, modulation_ref[1, :, columns], clips)
            modulated[:, columns] = (normed * (1.0 + scale) + shift).astype(jnp.bfloat16)

    hidden[...] = jax.nn.gelu(
        jnp.dot(modulated[...], w_in[...], preferred_element_type=jnp.float32), approximate=True
    ).astype(jnp.bfloat16)


def mlp_in(clips, order, ids, modulation, parts, w_in):
    rows = parts[0].shape[0]
    width, units = w_in.shape
    block = math.gcd(units, 512)
    return pl.pallas_call(
        functools.partial(mlp_in_kernel, clips, len(parts)),
        grid=(units // block,),
        out_shape=jax.ShapeDtypeStruct((rows, units), jnp.bfloat16),
        in_specs=[SMEM, VMEM, VMEM]
        + [VMEM] * len(parts)
        + [pl.BlockSpec((width, block), lambda i: (0, i))],
        out_specs=pl.BlockSpec((rows, block), lambda i: (0, i)),
        scratch_shapes=[pltpu.VMEM((rows, width), jnp.bfloat16)],
        compiler_params=params(MLP_GRANT),
        cost_estimate=cost(2 * rows * width * units, 2 * width * units),
        name="mlp_in",
    )(order, ids[:, None], modulation, *parts, w_in)


def mlp_out_kernel(hidden, w_out, branch):
    branch[...] = jnp.dot(hidden[...], w_out[...], preferred_element_type=jnp.float32)


def mlp_out(hidden, w_out):
    rows, units = hidden.shape
    width = w_out.shape[1]
    block = math.gcd(width, 512)
    return pl.pallas_call(
        mlp_out_kernel,
        grid=(width // block,),
        out_shape=jax.ShapeDtypeStruct((rows, width), jnp.float32),
        in_specs=[VMEM, pl.BlockSpec((units, block), lambda i: (0, i))],
        out_specs=pl.BlockSpec((rows, block), lambda i: (0, i)),
        compiler_params=params(MLP_GRANT),
        cost_estimate=cost(2 * rows * width * units, 2 * width * units + 4 * rows * width),
        name="mlp_out",
    )(hidden, w_out)


def project_kernel(ways, first, blocks, scalars, *refs):
    pieces = 2 * ways
    attended = refs[:pieces]
    w_hbm, mlp_hbm, kept, sent, gathered, w, branch, sems = refs[pieces:]
    half, width = kept.shape
    share = mlp_hbm.shape[0] // 2
    block = width // blocks
    copies = []
    for i in range(2):
        start = pl.multiple_of(scalars[pieces + i] * share + first, math.gcd(share, half))
        copies.append(
            pltpu.make_async_copy(mlp_hbm.at[pl.ds(start, half)], branch.at[i], sems.at[blocks + i])
        )
    for i in range(blocks):
        columns = slice(i * block, (i + 1) * block)
        copies.append(pltpu.make_async_copy(w_hbm.at[:, columns], w.at[:, columns], sems.at[i]))
    for copy in copies:
        copy.start()
    for i in range(pieces):
        columns = pl.ds(pl.multiple_of(scalars[i] * HD, HD), HD)
        gathered[:, columns] = attended[i][i // ways]
    mine = gathered[pl.ds(pl.multiple_of(scalars[pieces] * half, half), half), :]
    other = gathered[pl.ds(pl.multiple_of(scalars[pieces + 1] * half, half), half), :]
    copies[0].wait()
    copies[1].wait()
    for i in range(blocks):
        columns = slice(i * block, (i + 1) * block)
        copies[2 + i].wait()
        sent[:, columns] = (
            branch[1, :, columns]
            + jnp.dot(other, w[:, columns], preferred_element_type=jnp.float32)
        ).astype(jnp.bfloat16)
        kept[:, columns] = branch[0, :, columns] + jnp.dot(
            mine, w[:, columns], preferred_element_type=jnp.float32
        )


def project(scalars, attended, got, w_attn_out, mlp_branch, first, name):
    rows, width = mlp_branch.shape
    count = got[0].shape[1]
    ways, half = len(attended), count // 2
    inputs = w_attn_out.shape[0]
    blocks = width // math.gcd(width, 512)
    return pl.pallas_call(
        functools.partial(project_kernel, ways, first, blocks),
        out_shape=[
            jax.ShapeDtypeStruct((half, width), jnp.float32),
            jax.ShapeDtypeStruct((half, width), jnp.bfloat16),
        ],
        in_specs=[SMEM] + [VMEM] * (2 * ways) + [HBM, HBM],
        out_specs=[VMEM, VMEM],
        scratch_shapes=[
            pltpu.VMEM((count, inputs), jnp.bfloat16),
            pltpu.VMEM((inputs, width), jnp.bfloat16),
            pltpu.VMEM((2, half, width), jnp.float32),
            pltpu.SemaphoreType.DMA((blocks + 2,)),
        ],
        compiler_params=params(PROJECT_GRANT),
        cost_estimate=cost(2 * count * width * inputs, 2 * width * inputs + 4 * rows * width),
        name=name,
    )(scalars, *attended, *got, w_attn_out, mlp_branch)


def per_device(
    tokens,
    queries,
    key_rows,
    value_rows,
    clip_ids,
    causal,
    modulation,
    w_mlp,
    w_attn_out,
    w_mlp_out,
):
    local_rows = queries.shape[0]
    heads = queries.shape[1] // HD
    clips = causal.shape[0]
    tp_size = lax.axis_size("tp")
    ctx_size = lax.axis_size("ctx")
    here = lax.axis_index("ctx")
    tp_here = lax.axis_index("tp")
    first_row = here * local_rows
    own_ids = lax.dynamic_slice_in_dim(clip_ids, first_row, local_rows)
    clip_starts = jnp.sum(
        (clip_ids[None, :] < jnp.arange(clips + 1, dtype=jnp.int32)[:, None]).astype(jnp.int32),
        axis=1,
    )
    clip_scalars = jnp.concatenate([clip_starts, causal])
    share = local_rows // tp_size

    chips = ctx_size // 2
    split = (
        tp_size == 2
        and ctx_size % 2 == 0
        and chips & (chips - 1) == 0
        and heads == chips
        and local_rows == 3 * LANES
    )
    if split:
        return exchanged(
            tokens, queries, key_rows, value_rows, own_ids, clip_scalars, clips, modulation,
            w_mlp, w_attn_out, w_mlp_out, chips,
        )

    full_rows = lax.all_gather(tokens, "tp", axis=1, tiled=True)
    hidden = mlp_in(clips, jnp.zeros((1,), jnp.int32), own_ids, modulation, [full_rows], w_mlp)
    branch = mlp_out(hidden, w_mlp_out)
    all_keys = lax.all_gather(key_rows, "ctx", axis=0, tiled=True)
    all_values = lax.all_gather(value_rows, "ctx", axis=0, tiled=True)
    scalars = jnp.concatenate([clip_scalars, first_row[None]])
    kv_scalars = jnp.concatenate([clip_scalars, jnp.zeros((1,), jnp.int32)])
    attended = []
    for head in range(heads):
        columns = slice(head * HD, (head + 1) * HD)
        kv = jnp.stack([all_keys[:, columns], value_blocks(all_values[:, columns])])
        k, v = assemble(clips, kv_scalars, [kv[:, None]])
        attended.extend(
            attention(
                clips, scalars, [queries[None, None, :, columns]], 0, local_rows, k, v,
                local_rows // 2, "attention",
            )
        )
    branch = lax.psum_scatter(
        branch
        + jnp.dot(jnp.concatenate([one[0] for one in attended], axis=1), w_attn_out, preferred_element_type=jnp.float32),
        "tp",
        scatter_dimension=0,
        tiled=True,
    )
    residual = lax.dynamic_slice_in_dim(full_rows, tp_here * share, share, 0)
    share_ids = lax.dynamic_slice_in_dim(own_ids, tp_here * share, share)
    gate_rows = select_rows(share_ids[:, None], modulation[2], clips)
    return residual.astype(jnp.float32) + gate_rows * branch


def exchanged(
    tokens, queries, key_rows, value_rows, own_ids, clip_scalars, clips, modulation,
    w_mlp, w_attn_out, w_mlp_out, chips,
):
    local_rows = queries.shape[0]
    share = local_rows // 2
    here = lax.axis_index("ctx")
    tp_here = lax.axis_index("tp")
    order = jnp.stack([tp_here, 1 - tp_here])
    chip, core = here // 2, here % 2
    ways = chips // 2
    chunk_rows = (share, share)

    def swap_tp(array):
        return lax.ppermute(array, "tp", [(0, 1), (1, 0)])

    def swap_cores(array):
        pairs = [(2 * i + c, 2 * i + 1 - c) for i in range(chips) for c in (0, 1)]
        return lax.ppermute(array, "ctx", pairs)

    def exchange(array, m):
        pairs = [(2 * i + c, 2 * (i ^ (2 * m + c)) + c) for i in range(chips) for c in (0, 1)]
        return lax.ppermute(array, "ctx", pairs)

    def met_by(c):
        return [lax.bitwise_xor(chip, 2 * m + c) for m in range(ways)]

    mine, others = met_by(core), met_by(1 - core)
    other_half = swap_tp(tokens)
    keep, give = split_heads(
        jnp.stack(others + mine), ways, chunk_rows, queries, key_rows, value_rows
    )
    messages = pack(keep, swap_cores(give))
    own_pieces = [None] * ways
    for m in reversed(range(ways)):
        own_pieces[m] = exchange(messages[m], m)
    parts = [tokens, other_half]
    hidden = mlp_in(clips, order, own_ids, modulation, parts, w_mlp)
    for m in range(ways // 2):
        own_pieces[m], hidden = lax.optimization_barrier((own_pieces[m], hidden))
    mlp_branch = mlp_out(hidden, w_mlp_out)
    for m in range(ways // 2, ways):
        own_pieces[m], mlp_branch = lax.optimization_barrier((own_pieces[m], mlp_branch))
    core_pieces = [swap_cores(piece) for piece in own_pieces]

    def places(met, c):
        return [
            at * (2 * local_rows) + place * local_rows for at in met for place in (c, 1 - c)
        ]

    own_at = places(mine, core)
    kv_at = jnp.stack(own_at + places(others, 1 - core))
    k, v = assemble(
        clips, jnp.concatenate([clip_scalars, kv_at]), own_pieces + core_pieces
    )

    project_scalars = jnp.concatenate([jnp.stack(mine + others), order])
    attended = []
    query_at = jnp.stack(own_at)
    for chunk, rows in enumerate(chunk_rows):
        start = sum(chunk_rows[:chunk])
        scalars = jnp.concatenate([clip_scalars, query_at + start // 2])
        outs = attention(
            clips, scalars, own_pieces, start, rows, k, v, share, "attention_%d" % chunk
        )
        if chunk:
            outs, attended[-1] = lax.optimization_barrier((outs, attended[-1]))
        attended.append([exchange(piece, m) for m, piece in enumerate(outs)])
        query_at, outs = lax.optimization_barrier((query_at, outs[0]))
    mlp_branch, outs = lax.optimization_barrier((mlp_branch, outs))
    pieces = []
    for chunk, rows in enumerate(chunk_rows):
        got = [swap_cores(piece) for piece in attended[chunk]]
        kept, sent = project(
            project_scalars, attended[chunk], got, w_attn_out, mlp_branch,
            sum(chunk_rows[:chunk]) // 2, "project_%d" % chunk,
        )
        for later in range(chunk + 1, len(chunk_rows)):
            attended[later], sent = lax.optimization_barrier((attended[later], sent))
        pieces.append((kept, swap_tp(sent)))
    branch = jnp.concatenate([kept + came.astype(jnp.float32) for kept, came in pieces], axis=0)
    own = [lax.dynamic_slice_in_dim(part, tp_here * share, share, 0) for part in parts]
    residual = jnp.where(
        tp_here == 0, jnp.concatenate(own, axis=1), jnp.concatenate(own[::-1], axis=1)
    )
    share_ids = lax.dynamic_slice_in_dim(own_ids, tp_here * share, share)
    gate_rows = select_rows(share_ids[:, None], modulation[2], clips)
    return residual.astype(jnp.float32) + gate_rows * branch


def solution(mesh):
    in_specs = (
        P("ctx", "tp"),
        P("ctx", "tp"),
        P("ctx", "tp"),
        P("ctx", "tp"),
        P(),
        P(),
        P(),
        P(None, "tp"),
        P("tp", None),
        P("tp", None),
    )
    out_specs = P(("ctx", "tp"), None)
    return jax.shard_map(
        per_device, mesh=mesh, in_specs=in_specs, out_specs=out_specs, check_vma=False
    )
```

```python
import functools
import math

import jax
import jax.numpy as jnp
from jax import lax
from jax.experimental import pallas as pl
from jax.experimental.pallas import tpu as pltpu
from jax.sharding import PartitionSpec as P

HD = 128
LANES = 128
ONES_ROWS = 8
KEY_WIDTH = 2 * HD
MASKED = -3e38
COST_SCALE = 1
SPLIT_GRANT = 60
MLP_GRANT = 44
PROJECT_GRANT = 50
START_MAX = -1e30
EPS_NORM = 1e-06
EXP2_SCALE = math.log2(math.e) / math.sqrt(HD)

ANY = pl.BlockSpec(memory_space=pl.ANY)
HBM = pl.BlockSpec(memory_space=pltpu.HBM)
SMEM = pl.BlockSpec(memory_space=pltpu.SMEM)
VMEM = pl.BlockSpec(memory_space=pltpu.VMEM)


def params(mebibytes):
    return pltpu.CompilerParams(vmem_limit_bytes=mebibytes << 20)


def cost(flops, nbytes, exps=0):
    return pl.CostEstimate(
        flops=flops // COST_SCALE, bytes_accessed=nbytes // COST_SCALE, transcendentals=exps // COST_SCALE
    )


def met(place, m, other):
    core = lax.bitwise_xor(place[1], other)
    return lax.bitwise_xor(place[0], 2 * m + core)


def token_base(place, m, other, group, rows):
    core = lax.bitwise_xor(lax.bitwise_xor(place[1], other), group)
    return (met(place, m, other) * 2 + core) * rows


def split_kernel(
    ways, chunk_rows, place, q_hbm, k_hbm, v_hbm, keep, give, q, k, v, sems
):
    rows = q.shape[0]
    share = rows // 2
    copies = [
        pltpu.make_async_copy(source, target, sems.at[i])
        for i, (source, target) in enumerate(((k_hbm, k), (v_hbm, v), (q_hbm, q)))
    ]
    for copy in copies:
        copy.start()
    for copy in copies:
        copy.wait()
    for side, out in enumerate((give, keep)):
        for m in range(ways):
            head = met(place, m, 1 - side)
            columns = pl.ds(pl.multiple_of(head * HD, HD), HD)
            out[m, 0] = k[:, columns]
            for at in range(0, rows, LANES):
                block = v[at : at + LANES, columns].astype(jnp.float32)
                out[m, 1, at : at + LANES, :] = jnp.transpose(block).astype(jnp.bfloat16)
            first = 0
            for count in chunk_rows:
                half = count // 2
                start = 2 * first
                out[m, 2, start : start + half] = q[first : first + half, columns]
                out[m, 2, start + half : start + count] = q[
                    share + first : share + first + half, columns
                ]
                first += half


def split_heads(scalars, ways, chunk_rows, queries, key_rows, value_rows):
    rows = queries.shape[0]
    shape = jax.ShapeDtypeStruct((ways, 3, rows, HD), jnp.bfloat16)
    return pl.pallas_call(
        functools.partial(split_kernel, ways, chunk_rows),
        out_shape=[shape, shape],
        in_specs=[SMEM, HBM, HBM, HBM],
        out_specs=[VMEM, VMEM],
        scratch_shapes=[pltpu.VMEM(queries.shape, jnp.bfloat16)] * 3
        + [pltpu.SemaphoreType.DMA((3,))],
        compiler_params=params(SPLIT_GRANT),
        name="split_heads",
    )(scalars, queries, key_rows, value_rows)


def pack_kernel(ways, keep, got, *refs):
    outs, sems = refs[:ways], refs[ways]
    copies = []
    for m in reversed(range(ways)):
        for i, source in enumerate((keep, got)):
            copies.append(
                pltpu.make_async_copy(source.at[m], outs[m].at[:, i], sems.at[2 * m + i])
            )
            copies[-1].start()
    for copy in copies:
        copy.wait()


def pack(keep, got):
    ways, arrays, rows, _ = keep.shape
    return pl.pallas_call(
        functools.partial(pack_kernel, ways),
        out_shape=[jax.ShapeDtypeStruct((arrays, 2, rows, HD), jnp.bfloat16)] * ways,
        in_specs=[ANY, ANY],
        out_specs=[ANY] * ways,
        scratch_shapes=[pltpu.SemaphoreType.DMA((2 * ways,))],
        compiler_params=params(4),
        name="pack",
    )(keep, got)


def pick_kernel(ways, *refs):
    pieces, out, sems = refs[:ways], refs[ways], refs[ways + 1]
    copies = []
    for m in range(ways):
        copies.append(pltpu.make_async_copy(pieces[m].at[1], out.at[m], sems.at[m]))
        copies[-1].start()
    for copy in copies:
        copy.wait()


def pick_others(pieces):
    _, rows, width = pieces[0].shape
    return pl.pallas_call(
        functools.partial(pick_kernel, len(pieces)),
        out_shape=jax.ShapeDtypeStruct((len(pieces), rows, width), jnp.bfloat16),
        in_specs=[ANY] * len(pieces),
        out_specs=ANY,
        scratch_shapes=[pltpu.SemaphoreType.DMA((len(pieces),))],
        compiler_params=params(4),
        name="pick_others",
    )(*pieces)


def clip_lanes(scalars, clips):
    lane = lax.broadcasted_iota(jnp.int32, (1, HD), 1)
    low = jnp.zeros_like(lane)
    high = jnp.zeros_like(lane)
    for clip in range(clips):
        low = jnp.where(lane == clip, scalars[clip], low)
        high = jnp.where(lane == clip, scalars[clip + 1], high)
    return low, high


def assemble_kernel(clips, n_kv, exchanged_pieces, scalars, place, *refs):
    pieces = refs[:n_kv]
    k, v, sems = refs[n_kv:]
    all_keys = k.shape[0]
    copies = []

    def load(source, target):
        copies.append(pltpu.make_async_copy(source, target, sems.at[len(copies)]))
        copies[-1].start()

    for i, piece in enumerate(pieces):
        groups, count = piece.shape[1:3]
        for group in range(groups):
            base = 0
            if exchanged_pieces:
                ways = n_kv // 2
                base = token_base(place, i % ways, i // ways, group, count)
                base = pl.multiple_of(base, LANES)
            load(piece.at[0, group], k.at[pl.ds(base, count), 0:HD])
            for at in range(0, count, LANES):
                columns = pl.ds(pl.multiple_of(base + at, LANES), LANES)
                load(piece.at[1, group, at : at + LANES], v.at[0:HD, columns])
    low, high = clip_lanes(scalars, clips)
    step = math.gcd(all_keys, 768)
    for at in range(0, all_keys, step):
        pos = at + lax.broadcasted_iota(jnp.int32, (step, HD), 0)
        inside = (pos >= low) & (pos < high)
        k[at : at + step, HD:] = jnp.where(inside, 1.0, 0.0).astype(jnp.bfloat16)
    v[HD:, :] = jnp.ones((v.shape[0] - HD, all_keys), jnp.bfloat16)
    for copy in copies:
        copy.wait()


def assemble(clips, scalars, place, kv_pieces, exchanged_pieces):
    all_keys = sum(piece.shape[1] * piece.shape[2] for piece in kv_pieces)
    n_sems = sum(piece.shape[1] * (1 + piece.shape[2] // LANES) for piece in kv_pieces)
    return pl.pallas_call(
        functools.partial(assemble_kernel, clips, len(kv_pieces), exchanged_pieces),
        out_shape=[
            jax.ShapeDtypeStruct((all_keys, KEY_WIDTH), jnp.bfloat16),
            jax.ShapeDtypeStruct((HD + ONES_ROWS, all_keys), jnp.bfloat16),
        ],
        in_specs=[SMEM, SMEM] + [ANY] * len(kv_pieces),
        out_specs=[VMEM, VMEM],
        scratch_shapes=[pltpu.SemaphoreType.DMA((n_sems,))],
        compiler_params=params(16),
        name="assemble",
    )(scalars, place, *kv_pieces)


def span_of(scalars, clips, pos):
    low = jnp.zeros_like(pos)
    high = jnp.zeros_like(pos)
    for clip in range(clips):
        inside = pos >= scalars[clip]
        end = jnp.where(scalars[clips + 1 + clip] != 0, pos + 1, scalars[clip + 1])
        low = jnp.where(inside, scalars[clip], low)
        high = jnp.where(inside, end, high)
    return low, high


def attention_kernel(
    clips, share, start, key_tile, exchanged_pieces, scalars, place, k, v, *refs
):
    n_query = (len(refs) - 8) // 2
    query_hbm = refs[:n_query]
    out_hbm = refs[n_query : 2 * n_query]
    q, out, total, peak, score_a, score_b, block_peak, sems = refs[2 * n_query :]
    width = q.shape[1]
    groups, rows, _ = out_hbm[0].shape
    half = rows // 2
    none_causal = 1 << 30
    copies = []
    for i in range(n_query):
        arrays = query_hbm[i].shape[0]
        for group in range(groups):
            copies.append(
                pltpu.make_async_copy(
                    query_hbm[i].at[arrays - 1, group, start : start + rows],
                    q.at[i, group * rows : (group + 1) * rows, 0:HD],
                    sems.at[i * groups + group],
                )
            )
            copies[-1].start()
    clip_low, clip_high = clip_lanes(scalars, clips)
    for copy in copies:
        copy.wait()
    scores = [score_a, score_b]
    leaving = [
        [
            pltpu.make_async_copy(
                out.at[i, group * rows : (group + 1) * rows],
                out_hbm[i].at[group],
                sems.at[i * groups + group],
            )
            for group in range(groups)
        ]
        for i in range(n_query)
    ]

    def positions(shape, axis, firsts):
        index = lax.broadcasted_iota(jnp.int32, shape, axis)
        pos = index
        for group, first in enumerate(firsts):
            at = group * rows
            pos = jnp.where(index >= at, index + (first - at), pos)
            pos = jnp.where(index >= at + half, index + (first + share - at - half), pos)
        return pos

    def one_tile(piece, _):
        if exchanged_pieces:
            firsts = [
                token_base(place, piece, 0, group, 2 * share) + start // 2
                for group in range(groups)
            ]
        else:
            firsts = [place[0]]
        begin, end, causal_from = none_causal, 0, none_causal
        for first in firsts:
            last = first + share + half - 1
            begin = jnp.minimum(begin, span_of(scalars, clips, first)[0])
            end = jnp.maximum(end, span_of(scalars, clips, last)[1])
            for clip in range(clips):
                met = (first < scalars[clip + 1]) & (last >= scalars[clip])
                met = met & (scalars[clips + 1 + clip] != 0)
                causal_from = jnp.where(
                    met, jnp.minimum(causal_from, jnp.maximum(first, scalars[clip])), causal_from
                )
        begin = begin // key_tile
        end = (end + key_tile - 1) // key_tile
        pos = positions((1, width), 1, firsts)
        last_key = jnp.full_like(pos, none_causal)
        for clip in range(clips):
            inside = (pos >= scalars[clip]) & (pos < scalars[clip + 1])
            inside = inside & (scalars[clips + 1 + clip] != 0)
            last_key = jnp.where(inside, pos, last_key)
        row_pos = positions((width, HD), 0, firsts)
        inside = (row_pos >= clip_low) & (row_pos < clip_high)
        q[piece, :, HD:] = jnp.where(inside, 0.0, MASKED).astype(jnp.bfloat16)
        total[...] = jnp.zeros_like(total)
        peak[...] = jnp.full_like(peak, START_MAX)

        def multiply(tile, slot):
            keys = k[pl.ds(pl.multiple_of(tile * key_tile, key_tile), key_tile), :]
            block = lax.dot_general(
                keys, q[piece], (((1,), (1,)), ((), ())), preferred_element_type=jnp.float32
            )
            scores[slot][...] = block
            block_peak[slot] = jnp.max(block, axis=0, keepdims=True)

        def mask(tile, slot):
            @pl.when((tile + 1) * key_tile - 1 > causal_from)
            def _():
                key_pos = tile * key_tile + lax.broadcasted_iota(jnp.int32, (key_tile, 1), 0)
                block = jnp.where(key_pos <= last_key, scores[slot][...], MASKED)
                scores[slot][...] = block
                block_peak[slot] = jnp.max(block, axis=0, keepdims=True)

        def gather(tile, slot):
            old = peak[...]
            new = jnp.maximum(old, block_peak[slot])
            peak[...] = new
            factor = jnp.exp2((old - new) * EXP2_SCALE)
            weights = jnp.exp2(scores[slot][...] * EXP2_SCALE - new * EXP2_SCALE)
            values = v[:, pl.ds(pl.multiple_of(tile * key_tile, key_tile), key_tile)]
            total[...] = total[...] * factor + jnp.dot(
                values, weights.astype(jnp.bfloat16), preferred_element_type=jnp.float32
            )

        multiply(begin, 0)
        mask(begin, 0)
        count = end - begin

        def two_tiles(pair, _):
            tile = begin + 2 * pair
            multiply(tile + 1, 1)
            gather(tile, 0)
            mask(tile + 1, 1)
            later = jnp.minimum(tile + 2, end - 1)
            multiply(later, 0)
            gather(tile + 1, 1)
            mask(later, 0)
            return 0

        lax.fori_loop(0, count // 2, two_tiles, 0)

        @pl.when(count % 2 == 1)
        def _():
            gather(end - 1, 0)

        both = total[...]
        out[piece] = jnp.transpose(both[:HD] / both[HD : HD + 1]).astype(jnp.bfloat16)
        return 0

    def tile_and_leave(piece, _):
        one_tile(piece, _)
        for i in range(n_query):

            @pl.when(piece == i)
            def _():
                for copy in leaving[i]:
                    copy.start()

        return 0

    lax.fori_loop(0, n_query, tile_and_leave, 0)
    for some in leaving:
        for copy in some:
            copy.wait()


def attention(
    clips, scalars, place, queries, start, rows, k, v, share, exchanged_pieces, name
):
    n_query = len(queries)
    groups = queries[0].shape[1]
    width = groups * rows
    all_keys = k.shape[0]
    key_tile = math.gcd(all_keys, 768)
    return pl.pallas_call(
        functools.partial(
            attention_kernel, clips, share, start, key_tile, exchanged_pieces
        ),
        out_shape=[jax.ShapeDtypeStruct((groups, rows, HD), jnp.bfloat16)] * n_query,
        in_specs=[SMEM, SMEM, VMEM, VMEM] + [ANY] * n_query,
        out_specs=[ANY] * n_query,
        scratch_shapes=[
            pltpu.VMEM((n_query, width, KEY_WIDTH), jnp.bfloat16),
            pltpu.VMEM((n_query, width, HD), jnp.bfloat16),
            pltpu.VMEM((HD + ONES_ROWS, width), jnp.float32),
            pltpu.VMEM((1, width), jnp.float32),
            pltpu.VMEM((key_tile, width), jnp.float32),
            pltpu.VMEM((key_tile, width), jnp.float32),
            pltpu.VMEM((2, 1, width), jnp.float32),
            pltpu.SemaphoreType.DMA((n_query * groups,)),
        ],
        compiler_params=params(20),
        cost_estimate=cost(
            4 * n_query * width * all_keys * HD, 4 * all_keys * HD, n_query * width * all_keys
        ),
        name=name,
    )(scalars, place, k, v, *queries)


def value_blocks(values):
    count = values.shape[0]
    return jnp.swapaxes(values.reshape(count // LANES, LANES, HD), 1, 2).reshape(count, HD)


def select_rows(ids, table, clips):
    picked = jnp.broadcast_to(table[0:1], (ids.shape[0], table.shape[1]))
    for clip in range(1, clips):
        picked = jnp.where(ids == clip, table[clip : clip + 1], picked)
    return picked


def mlp_in_kernel(clips, n_parts, place, ids_ref, modulation_ref, *refs):
    parts = refs[:n_parts]
    w_in, hidden, modulated = refs[n_parts:]
    width = modulated.shape[1]

    @pl.when(pl.program_id(0) == 0)
    def _():
        part_width = width // n_parts
        mean = sum(
            jnp.sum(part[...].astype(jnp.float32), axis=1, keepdims=True) for part in parts
        ) / width
        variance = sum(
            jnp.sum((part[...].astype(jnp.float32) - mean) ** 2, axis=1, keepdims=True)
            for part in parts
        ) / width
        inverse = lax.rsqrt(variance + EPS_NORM)
        ids = ids_ref[...]
        for i, part in enumerate(parts):
            part_at = lax.bitwise_xor(place[2], i) if n_parts > 1 else 0
            columns = pl.ds(pl.multiple_of(part_at * part_width, LANES), part_width)
            normed = (part[...].astype(jnp.float32) - mean) * inverse
            shift = select_rows(ids, modulation_ref[0, :, columns], clips)
            scale = select_rows(ids, modulation_ref[1, :, columns], clips)
            modulated[:, columns] = (normed * (1.0 + scale) + shift).astype(jnp.bfloat16)

    hidden[...] = jax.nn.gelu(
        jnp.dot(modulated[...], w_in[...], preferred_element_type=jnp.float32), approximate=True
    ).astype(jnp.bfloat16)


def mlp_in(clips, order, ids, modulation, parts, w_in):
    rows = parts[0].shape[0]
    width, units = w_in.shape
    block = math.gcd(units, 512)
    return pl.pallas_call(
        functools.partial(mlp_in_kernel, clips, len(parts)),
        grid=(units // block,),
        out_shape=jax.ShapeDtypeStruct((rows, units), jnp.bfloat16),
        in_specs=[SMEM, VMEM, VMEM]
        + [VMEM] * len(parts)
        + [pl.BlockSpec((width, block), lambda i: (0, i))],
        out_specs=pl.BlockSpec((rows, block), lambda i: (0, i)),
        scratch_shapes=[pltpu.VMEM((rows, width), jnp.bfloat16)],
        compiler_params=params(MLP_GRANT),
        cost_estimate=cost(2 * rows * width * units, 2 * width * units),
        name="mlp_in",
    )(order, ids[:, None], modulation, *parts, w_in)


def mlp_out_kernel(hidden, w_out, branch):
    branch[...] = jnp.dot(hidden[...], w_out[...], preferred_element_type=jnp.float32)


def mlp_out(hidden, w_out):
    rows, units = hidden.shape
    width = w_out.shape[1]
    block = math.gcd(width, 512)
    return pl.pallas_call(
        mlp_out_kernel,
        grid=(width // block,),
        out_shape=jax.ShapeDtypeStruct((rows, width), jnp.float32),
        in_specs=[VMEM, pl.BlockSpec((units, block), lambda i: (0, i))],
        out_specs=pl.BlockSpec((rows, block), lambda i: (0, i)),
        compiler_params=params(MLP_GRANT),
        cost_estimate=cost(2 * rows * width * units, 2 * width * units + 4 * rows * width),
        name="mlp_out",
    )(hidden, w_out)


def project_kernel(ways, first, side, blocks, place, *refs):
    pieces = 2 * ways
    attended = refs[:ways]
    got, w_hbm, mlp_hbm, out, gathered, w, branch, sems = refs[ways:]
    half, width = out.shape
    share = mlp_hbm.shape[0] // 2
    block = width // blocks
    owner = lax.bitwise_xor(place[2], side)
    start = pl.multiple_of(owner * share + first, math.gcd(share, half))
    rows = pltpu.make_async_copy(mlp_hbm.at[pl.ds(start, half)], branch, sems.at[blocks])
    copies = []
    for i in range(blocks):
        columns = slice(i * block, (i + 1) * block)
        copies.append(pltpu.make_async_copy(w_hbm.at[:, columns], w.at[:, columns], sems.at[i]))
    for copy in [copies[0], rows] + copies[1:]:
        copy.start()
    at = pl.multiple_of(owner * half, half)
    for i in range(pieces):
        head = met(place, i % ways, i // ways)
        columns = pl.ds(pl.multiple_of(head * HD, HD), HD)
        if i < ways:
            gathered[:, columns] = attended[i][0, pl.ds(at, half), :]
        else:
            gathered[:, columns] = got[i - ways, pl.ds(at, half), :]
    for i in range(blocks):
        columns = slice(i * block, (i + 1) * block)
        copies[i].wait()
        product = jnp.dot(gathered[...], w[:, columns], preferred_element_type=jnp.float32)
        if i == 0:
            rows.wait()
        out[:, columns] = (branch[:, columns] + product).astype(out.dtype)


def project(scalars, attended, got, w_attn_out, mlp_branch, first, side, dtype, name):
    width = mlp_branch.shape[1]
    ways, half = len(attended), got.shape[1] // 2
    inputs = w_attn_out.shape[0]
    blocks = width // math.gcd(width, 768)
    return pl.pallas_call(
        functools.partial(project_kernel, ways, first, side, blocks),
        out_shape=jax.ShapeDtypeStruct((half, width), dtype),
        in_specs=[SMEM] + [VMEM] * (ways + 1) + [HBM, HBM],
        out_specs=VMEM,
        scratch_shapes=[
            pltpu.VMEM((half, inputs), jnp.bfloat16),
            pltpu.VMEM((inputs, width), jnp.bfloat16),
            pltpu.VMEM((half, width), jnp.float32),
            pltpu.SemaphoreType.DMA((blocks + 1,)),
        ],
        compiler_params=params(PROJECT_GRANT),
        cost_estimate=cost(1, 1),
        name=name,
    )(scalars, *attended, got, w_attn_out, mlp_branch)


def per_device(
    tokens,
    queries,
    key_rows,
    value_rows,
    clip_ids,
    causal,
    modulation,
    w_mlp,
    w_attn_out,
    w_mlp_out,
):
    local_rows = queries.shape[0]
    heads = queries.shape[1] // HD
    clips = causal.shape[0]
    tp_size = lax.axis_size("tp")
    ctx_size = lax.axis_size("ctx")
    here = lax.axis_index("ctx")
    tp_here = lax.axis_index("tp")
    first_row = here * local_rows
    own_ids = lax.dynamic_slice_in_dim(clip_ids, first_row, local_rows)
    clip_starts = jnp.sum(
        (clip_ids[None, :] < jnp.arange(clips + 1, dtype=jnp.int32)[:, None]).astype(jnp.int32),
        axis=1,
    )
    clip_scalars = jnp.concatenate([clip_starts, causal])
    share = local_rows // tp_size

    chips = ctx_size // 2
    split = (
        tp_size == 2
        and ctx_size % 2 == 0
        and chips & (chips - 1) == 0
        and heads == chips
        and local_rows == 3 * LANES
    )
    if split:
        return exchanged(
            tokens, queries, key_rows, value_rows, own_ids, clip_scalars, clips, modulation,
            w_mlp, w_attn_out, w_mlp_out, chips,
        )

    place = jnp.stack([first_row, 0, tp_here])
    full_rows = lax.all_gather(tokens, "tp", axis=1, tiled=True)
    hidden = mlp_in(clips, place, own_ids, modulation, [full_rows], w_mlp)
    branch = mlp_out(hidden, w_mlp_out)
    all_keys = lax.all_gather(key_rows, "ctx", axis=0, tiled=True)
    all_values = lax.all_gather(value_rows, "ctx", axis=0, tiled=True)
    attended = []
    for head in range(heads):
        columns = slice(head * HD, (head + 1) * HD)
        kv = jnp.stack([all_keys[:, columns], value_blocks(all_values[:, columns])])
        k, v = assemble(clips, clip_scalars, place, [kv[:, None]], False)
        attended.extend(
            attention(
                clips, clip_scalars, place, [queries[None, None, :, columns]], 0, local_rows,
                k, v, local_rows // 2, False, "attention",
            )
        )
    branch = lax.psum_scatter(
        branch
        + jnp.dot(jnp.concatenate([one[0] for one in attended], axis=1), w_attn_out, preferred_element_type=jnp.float32),
        "tp",
        scatter_dimension=0,
        tiled=True,
    )
    residual = lax.dynamic_slice_in_dim(full_rows, tp_here * share, share, 0)
    share_ids = lax.dynamic_slice_in_dim(own_ids, tp_here * share, share)
    gate_rows = select_rows(share_ids[:, None], modulation[2], clips)
    return residual.astype(jnp.float32) + gate_rows * branch


def exchanged(
    tokens, queries, key_rows, value_rows, own_ids, clip_scalars, clips, modulation,
    w_mlp, w_attn_out, w_mlp_out, chips,
):
    local_rows = queries.shape[0]
    share = local_rows // 2
    here = lax.axis_index("ctx")
    tp_here = lax.axis_index("tp")
    ways = chips // 2
    chunk_rows = (2 * LANES, LANES)

    def swap_tp(array):
        return lax.ppermute(array, "tp", [(0, 1), (1, 0)])

    def swap_cores(array):
        pairs = [(2 * i + c, 2 * i + 1 - c) for i in range(chips) for c in (0, 1)]
        return lax.ppermute(array, "ctx", pairs)

    def exchange(array, m):
        pairs = [(2 * i + c, 2 * (i ^ (2 * m + c)) + c) for i in range(chips) for c in (0, 1)]
        return lax.ppermute(array, "ctx", pairs)

    place = jnp.stack([here // 2, here % 2, tp_here])
    other_half = swap_tp(tokens)
    keep, give = split_heads(
        place, ways, chunk_rows, queries, key_rows, value_rows
    )
    messages = pack(keep, swap_cores(give))
    own_pieces = [None] * ways
    for m in reversed(range(ways)):
        own_pieces[m] = exchange(messages[m], m)
    parts = [tokens, other_half]
    hidden = mlp_in(clips, place, own_ids, modulation, parts, w_mlp)
    mlp_branch = mlp_out(hidden, w_mlp_out)
    for m in reversed(range(ways)):
        own_pieces[m], mlp_branch = lax.optimization_barrier((own_pieces[m], mlp_branch))
    core_pieces = [swap_cores(piece) for piece in own_pieces]

    k, v = assemble(clips, clip_scalars, place, own_pieces + core_pieces, True)

    def attend(chunk):
        start = sum(chunk_rows[:chunk])
        return attention(
            clips, clip_scalars, place, own_pieces, start, chunk_rows[chunk], k, v, share, True,
            "attention_%d" % chunk,
        )

    def send_back(outs):
        return [exchange(piece, m) for m, piece in enumerate(outs)]

    def kept_rows(chunk, attended, got):
        return project(
            place, attended, got, w_attn_out, mlp_branch,
            sum(chunk_rows[:chunk]) // 2, 0, jnp.float32, "project_kept_%d" % chunk,
        )

    def sent_rows(chunk, attended, got):
        return project(
            place, attended, got, w_attn_out, mlp_branch,
            sum(chunk_rows[:chunk]) // 2, 1, jnp.bfloat16, "project_sent_%d" % chunk,
        )

    first_outs = attend(0)
    first = send_back(first_outs)
    clip_scalars, _ = lax.optimization_barrier((clip_scalars, first_outs[0]))
    second_outs = attend(1)
    first, second_outs = lax.optimization_barrier((first, second_outs))
    first_got = swap_cores(pick_others(first))
    first_sent = sent_rows(0, first, first_got)
    second_outs, first_sent = lax.optimization_barrier((second_outs, first_sent))
    first_came = swap_tp(first_sent)
    second = send_back(second_outs)
    first, second_outs = lax.optimization_barrier((first, second_outs))
    first_kept = kept_rows(0, first, first_got)
    second, first_kept = lax.optimization_barrier((second, first_kept))
    second_got = swap_cores(pick_others(second))
    second_sent = sent_rows(1, second, second_got)
    second_sent, first_came = lax.optimization_barrier((second_sent, first_came))
    second_came = swap_tp(second_sent)
    tokens, other_half, own_ids, second, second_sent = lax.optimization_barrier(
        (tokens, other_half, own_ids, second, second_sent)
    )
    second_kept = kept_rows(1, second, second_got)
    own = [
        lax.dynamic_slice_in_dim(part, tp_here * share, share, 0) for part in (tokens, other_half)
    ]
    residual = jnp.where(
        tp_here == 0, jnp.concatenate(own, axis=1), jnp.concatenate(own[::-1], axis=1)
    ).astype(jnp.float32)
    share_ids = lax.dynamic_slice_in_dim(own_ids, tp_here * share, share)
    gate_rows = select_rows(share_ids[:, None], modulation[2], clips)
    cut = first_kept.shape[0]
    begun = residual[:cut] + gate_rows[:cut] * (first_kept + first_came.astype(jnp.float32))
    rest = residual[cut:] + gate_rows[cut:] * second_kept
    begun, rest, gate_rest = lax.optimization_barrier((begun, rest, gate_rows[cut:]))
    rest = rest + gate_rest * second_came.astype(jnp.float32)
    return jnp.concatenate([begun, rest], axis=0)


def solution(mesh):
    in_specs = (
        P("ctx", "tp"),
        P("ctx", "tp"),
        P("ctx", "tp"),
        P("ctx", "tp"),
        P(),
        P(),
        P(),
        P(None, "tp"),
        P("tp", None),
        P("tp", None),
    )
    out_specs = P(("ctx", "tp"), None)
    return jax.shard_map(
        per_device, mesh=mesh, in_specs=in_specs, out_specs=out_specs, check_vma=False
    )
```

```python
import functools
import math

import jax
import jax.numpy as jnp
from jax import lax
from jax.experimental import pallas as pl
from jax.experimental.pallas import tpu as pltpu
from jax.sharding import PartitionSpec as P

HD = 128
LANES = 128
ONES_ROWS = 8
KEY_WIDTH = 2 * HD
MASKED = -3e38
COST_SCALE = 1
SPLIT_GRANT = 60
MLP_GRANT = 44
PROJECT_GRANT = 50
START_MAX = -1e30
EPS_NORM = 1e-06
EXP2_SCALE = math.log2(math.e) / math.sqrt(HD)

ANY = pl.BlockSpec(memory_space=pl.ANY)
HBM = pl.BlockSpec(memory_space=pltpu.HBM)
SMEM = pl.BlockSpec(memory_space=pltpu.SMEM)
VMEM = pl.BlockSpec(memory_space=pltpu.VMEM)


def params(mebibytes):
    return pltpu.CompilerParams(vmem_limit_bytes=mebibytes << 20)


def cost(flops, nbytes, exps=0):
    return pl.CostEstimate(
        flops=flops // COST_SCALE, bytes_accessed=nbytes // COST_SCALE, transcendentals=exps // COST_SCALE
    )


def met(place, m, other):
    core = lax.bitwise_xor(place[1], other)
    return lax.bitwise_xor(place[0], 2 * m + core)


def token_base(place, m, other, group, rows):
    core = lax.bitwise_xor(lax.bitwise_xor(place[1], other), group)
    return (met(place, m, other) * 2 + core) * rows


def split_kernel(
    ways, chunk_rows, place, q_hbm, k_hbm, v_hbm, keep, give, q, k, v, sems
):
    rows = q.shape[0]
    share = rows // 2
    copies = [
        pltpu.make_async_copy(source, target, sems.at[i])
        for i, (source, target) in enumerate(((k_hbm, k), (v_hbm, v), (q_hbm, q)))
    ]
    for copy in copies:
        copy.start()
    for copy in copies:
        copy.wait()
    for side, out in enumerate((give, keep)):
        for m in range(ways):
            head = met(place, m, 1 - side)
            columns = pl.ds(pl.multiple_of(head * HD, HD), HD)
            out[m, 0] = k[:, columns]
            for at in range(0, rows, LANES):
                block = v[at : at + LANES, columns].astype(jnp.float32)
                out[m, 1, at : at + LANES, :] = jnp.transpose(block).astype(jnp.bfloat16)
            first = 0
            for count in chunk_rows:
                half = count // 2
                start = 2 * first
                out[m, 2, start : start + half] = q[first : first + half, columns]
                out[m, 2, start + half : start + count] = q[
                    share + first : share + first + half, columns
                ]
                first += half


def split_heads(scalars, ways, chunk_rows, queries, key_rows, value_rows):
    rows = queries.shape[0]
    shape = jax.ShapeDtypeStruct((ways, 3, rows, HD), jnp.bfloat16)
    return pl.pallas_call(
        functools.partial(split_kernel, ways, chunk_rows),
        out_shape=[shape, shape],
        in_specs=[SMEM, HBM, HBM, HBM],
        out_specs=[VMEM, VMEM],
        scratch_shapes=[pltpu.VMEM(queries.shape, jnp.bfloat16)] * 3
        + [pltpu.SemaphoreType.DMA((3,))],
        compiler_params=params(SPLIT_GRANT),
        name="split_heads",
    )(scalars, queries, key_rows, value_rows)


def pack_kernel(ways, keep, got, *refs):
    outs, sems = refs[:ways], refs[ways]
    copies = []
    for m in reversed(range(ways)):
        for i, source in enumerate((keep, got)):
            copies.append(
                pltpu.make_async_copy(source.at[m], outs[m].at[:, i], sems.at[2 * m + i])
            )
            copies[-1].start()
    for copy in copies:
        copy.wait()


def pack(keep, got):
    ways, arrays, rows, _ = keep.shape
    return pl.pallas_call(
        functools.partial(pack_kernel, ways),
        out_shape=[jax.ShapeDtypeStruct((arrays, 2, rows, HD), jnp.bfloat16)] * ways,
        in_specs=[ANY, ANY],
        out_specs=[ANY] * ways,
        scratch_shapes=[pltpu.SemaphoreType.DMA((2 * ways,))],
        compiler_params=params(4),
        name="pack",
    )(keep, got)


def pick_kernel(ways, *refs):
    pieces, out, sems = refs[:ways], refs[ways], refs[ways + 1]
    copies = []
    for m in range(ways):
        copies.append(pltpu.make_async_copy(pieces[m].at[1], out.at[m], sems.at[m]))
        copies[-1].start()
    for copy in copies:
        copy.wait()


def pick_others(pieces):
    _, rows, width = pieces[0].shape
    return pl.pallas_call(
        functools.partial(pick_kernel, len(pieces)),
        out_shape=jax.ShapeDtypeStruct((len(pieces), rows, width), jnp.bfloat16),
        in_specs=[ANY] * len(pieces),
        out_specs=ANY,
        scratch_shapes=[pltpu.SemaphoreType.DMA((len(pieces),))],
        compiler_params=params(4),
        name="pick_others",
    )(*pieces)


def clip_lanes(scalars, clips):
    lane = lax.broadcasted_iota(jnp.int32, (1, HD), 1)
    low = jnp.zeros_like(lane)
    high = jnp.zeros_like(lane)
    for clip in range(clips):
        low = jnp.where(lane == clip, scalars[clip], low)
        high = jnp.where(lane == clip, scalars[clip + 1], high)
    return low, high


def assemble_kernel(clips, n_kv, exchanged_pieces, scalars, place, *refs):
    pieces = refs[:n_kv]
    k, v, sems = refs[n_kv:]
    all_keys = k.shape[0]
    copies = []

    def load(source, target):
        copies.append(pltpu.make_async_copy(source, target, sems.at[len(copies)]))
        copies[-1].start()

    for i, piece in enumerate(pieces):
        groups, count = piece.shape[1:3]
        for group in range(groups):
            base = 0
            if exchanged_pieces:
                ways = n_kv // 2
                base = token_base(place, i % ways, i // ways, group, count)
                base = pl.multiple_of(base, LANES)
            load(piece.at[0, group], k.at[pl.ds(base, count), 0:HD])
            for at in range(0, count, LANES):
                columns = pl.ds(pl.multiple_of(base + at, LANES), LANES)
                load(piece.at[1, group, at : at + LANES], v.at[0:HD, columns])
    low, high = clip_lanes(scalars, clips)
    step = math.gcd(all_keys, 768)
    for at in range(0, all_keys, step):
        pos = at + lax.broadcasted_iota(jnp.int32, (step, HD), 0)
        inside = (pos >= low) & (pos < high)
        k[at : at + step, HD:] = jnp.where(inside, 1.0, 0.0).astype(jnp.bfloat16)
    v[HD:, :] = jnp.ones((v.shape[0] - HD, all_keys), jnp.bfloat16)
    for copy in copies:
        copy.wait()


def assemble(clips, scalars, place, kv_pieces, exchanged_pieces):
    all_keys = sum(piece.shape[1] * piece.shape[2] for piece in kv_pieces)
    n_sems = sum(piece.shape[1] * (1 + piece.shape[2] // LANES) for piece in kv_pieces)
    return pl.pallas_call(
        functools.partial(assemble_kernel, clips, len(kv_pieces), exchanged_pieces),
        out_shape=[
            jax.ShapeDtypeStruct((all_keys, KEY_WIDTH), jnp.bfloat16),
            jax.ShapeDtypeStruct((HD + ONES_ROWS, all_keys), jnp.bfloat16),
        ],
        in_specs=[SMEM, SMEM] + [ANY] * len(kv_pieces),
        out_specs=[VMEM, VMEM],
        scratch_shapes=[pltpu.SemaphoreType.DMA((n_sems,))],
        compiler_params=params(16),
        name="assemble",
    )(scalars, place, *kv_pieces)


def span_of(scalars, clips, pos):
    low = jnp.zeros_like(pos)
    high = jnp.zeros_like(pos)
    for clip in range(clips):
        inside = pos >= scalars[clip]
        end = jnp.where(scalars[clips + 1 + clip] != 0, pos + 1, scalars[clip + 1])
        low = jnp.where(inside, scalars[clip], low)
        high = jnp.where(inside, end, high)
    return low, high


def attention_kernel(
    clips, share, start, key_tile, first_way, scalars, place, k, v, *refs
):
    n_query = (len(refs) - 8) // 2
    query_hbm = refs[:n_query]
    out_hbm = refs[n_query : 2 * n_query]
    q, out, total, peak, score_a, score_b, block_peak, sems = refs[2 * n_query :]
    width = q.shape[1]
    groups, rows, _ = out_hbm[0].shape
    half = rows // 2
    none_causal = 1 << 30
    copies = []
    for i in range(n_query):
        arrays = query_hbm[i].shape[0]
        for group in range(groups):
            copies.append(
                pltpu.make_async_copy(
                    query_hbm[i].at[arrays - 1, group, start : start + rows],
                    q.at[i, group * rows : (group + 1) * rows, 0:HD],
                    sems.at[i * groups + group],
                )
            )
            copies[-1].start()
    clip_low, clip_high = clip_lanes(scalars, clips)
    for copy in copies:
        copy.wait()
    scores = [score_a, score_b]
    leaving = [
        [
            pltpu.make_async_copy(
                out.at[i, group * rows : (group + 1) * rows],
                out_hbm[i].at[group],
                sems.at[i * groups + group],
            )
            for group in range(groups)
        ]
        for i in range(n_query)
    ]

    def positions(shape, axis, firsts):
        index = lax.broadcasted_iota(jnp.int32, shape, axis)
        pos = index
        for group, first in enumerate(firsts):
            at = group * rows
            pos = jnp.where(index >= at, index + (first - at), pos)
            pos = jnp.where(index >= at + half, index + (first + share - at - half), pos)
        return pos

    def one_tile(piece, _):
        if first_way is not None:
            firsts = [
                token_base(place, first_way + piece, 0, group, 2 * share) + start // 2
                for group in range(groups)
            ]
        else:
            firsts = [place[0]]
        begin, end, causal_from = none_causal, 0, none_causal
        for first in firsts:
            last = first + share + half - 1
            begin = jnp.minimum(begin, span_of(scalars, clips, first)[0])
            end = jnp.maximum(end, span_of(scalars, clips, last)[1])
            for clip in range(clips):
                met = (first < scalars[clip + 1]) & (last >= scalars[clip])
                met = met & (scalars[clips + 1 + clip] != 0)
                causal_from = jnp.where(
                    met, jnp.minimum(causal_from, jnp.maximum(first, scalars[clip])), causal_from
                )
        begin = begin // key_tile
        end = (end + key_tile - 1) // key_tile
        pos = positions((1, width), 1, firsts)
        last_key = jnp.full_like(pos, none_causal)
        for clip in range(clips):
            inside = (pos >= scalars[clip]) & (pos < scalars[clip + 1])
            inside = inside & (scalars[clips + 1 + clip] != 0)
            last_key = jnp.where(inside, pos, last_key)
        row_pos = positions((width, HD), 0, firsts)
        inside = (row_pos >= clip_low) & (row_pos < clip_high)
        q[piece, :, HD:] = jnp.where(inside, 0.0, MASKED).astype(jnp.bfloat16)
        total[...] = jnp.zeros_like(total)
        peak[...] = jnp.full_like(peak, START_MAX)

        def multiply(tile, slot):
            keys = k[pl.ds(pl.multiple_of(tile * key_tile, key_tile), key_tile), :]
            block = lax.dot_general(
                keys, q[piece], (((1,), (1,)), ((), ())), preferred_element_type=jnp.float32
            )
            scores[slot][...] = block
            block_peak[slot] = jnp.max(block, axis=0, keepdims=True)

        def mask(tile, slot):
            @pl.when((tile + 1) * key_tile - 1 > causal_from)
            def _():
                key_pos = tile * key_tile + lax.broadcasted_iota(jnp.int32, (key_tile, 1), 0)
                block = jnp.where(key_pos <= last_key, scores[slot][...], MASKED)
                scores[slot][...] = block
                block_peak[slot] = jnp.max(block, axis=0, keepdims=True)

        def gather(tile, slot):
            old = peak[...]
            new = jnp.maximum(old, block_peak[slot])
            peak[...] = new
            factor = jnp.exp2((old - new) * EXP2_SCALE)
            weights = jnp.exp2(scores[slot][...] * EXP2_SCALE - new * EXP2_SCALE)
            values = v[:, pl.ds(pl.multiple_of(tile * key_tile, key_tile), key_tile)]
            total[...] = total[...] * factor + jnp.dot(
                values, weights.astype(jnp.bfloat16), preferred_element_type=jnp.float32
            )

        multiply(begin, 0)
        mask(begin, 0)
        count = end - begin

        def two_tiles(pair, _):
            tile = begin + 2 * pair
            multiply(tile + 1, 1)
            gather(tile, 0)
            mask(tile + 1, 1)
            later = jnp.minimum(tile + 2, end - 1)
            multiply(later, 0)
            gather(tile + 1, 1)
            mask(later, 0)
            return 0

        lax.fori_loop(0, count // 2, two_tiles, 0)

        @pl.when(count % 2 == 1)
        def _():
            gather(end - 1, 0)

        both = total[...]
        out[piece] = jnp.transpose(both[:HD] / both[HD : HD + 1]).astype(jnp.bfloat16)
        return 0

    def tile_and_leave(piece, _):
        one_tile(piece, _)
        for i in range(n_query):

            @pl.when(piece == i)
            def _():
                for copy in leaving[i]:
                    copy.start()

        return 0

    lax.fori_loop(0, n_query, tile_and_leave, 0)
    for some in leaving:
        for copy in some:
            copy.wait()


def attention(
    clips, scalars, place, queries, start, rows, k, v, share, first_way, name
):
    n_query = len(queries)
    groups = queries[0].shape[1]
    width = groups * rows
    all_keys = k.shape[0]
    key_tile = math.gcd(all_keys, 768)
    return pl.pallas_call(
        functools.partial(
            attention_kernel, clips, share, start, key_tile, first_way
        ),
        out_shape=[jax.ShapeDtypeStruct((groups, rows, HD), jnp.bfloat16)] * n_query,
        in_specs=[SMEM, SMEM, VMEM, VMEM] + [ANY] * n_query,
        out_specs=[ANY] * n_query,
        scratch_shapes=[
            pltpu.VMEM((n_query, width, KEY_WIDTH), jnp.bfloat16),
            pltpu.VMEM((n_query, width, HD), jnp.bfloat16),
            pltpu.VMEM((HD + ONES_ROWS, width), jnp.float32),
            pltpu.VMEM((1, width), jnp.float32),
            pltpu.VMEM((key_tile, width), jnp.float32),
            pltpu.VMEM((key_tile, width), jnp.float32),
            pltpu.VMEM((2, 1, width), jnp.float32),
            pltpu.SemaphoreType.DMA((n_query * groups,)),
        ],
        compiler_params=params(20),
        cost_estimate=cost(
            4 * n_query * width * all_keys * HD, 4 * all_keys * HD, n_query * width * all_keys
        ),
        name=name,
    )(scalars, place, k, v, *queries)


def value_blocks(values):
    count = values.shape[0]
    return jnp.swapaxes(values.reshape(count // LANES, LANES, HD), 1, 2).reshape(count, HD)


def select_rows(ids, table, clips):
    picked = jnp.broadcast_to(table[0:1], (ids.shape[0], table.shape[1]))
    for clip in range(1, clips):
        picked = jnp.where(ids == clip, table[clip : clip + 1], picked)
    return picked


def mlp_in_kernel(clips, n_parts, place, ids_ref, modulation_ref, *refs):
    parts = refs[:n_parts]
    w_in, hidden, modulated = refs[n_parts:]
    width = modulated.shape[1]

    @pl.when(pl.program_id(0) == 0)
    def _():
        part_width = width // n_parts
        mean = sum(
            jnp.sum(part[...].astype(jnp.float32), axis=1, keepdims=True) for part in parts
        ) / width
        variance = sum(
            jnp.sum((part[...].astype(jnp.float32) - mean) ** 2, axis=1, keepdims=True)
            for part in parts
        ) / width
        inverse = lax.rsqrt(variance + EPS_NORM)
        ids = ids_ref[...]
        for i, part in enumerate(parts):
            part_at = lax.bitwise_xor(place[2], i) if n_parts > 1 else 0
            columns = pl.ds(pl.multiple_of(part_at * part_width, LANES), part_width)
            normed = (part[...].astype(jnp.float32) - mean) * inverse
            shift = select_rows(ids, modulation_ref[0, :, columns], clips)
            scale = select_rows(ids, modulation_ref[1, :, columns], clips)
            modulated[:, columns] = (normed * (1.0 + scale) + shift).astype(jnp.bfloat16)

    hidden[...] = jax.nn.gelu(
        jnp.dot(modulated[...], w_in[...], preferred_element_type=jnp.float32), approximate=True
    ).astype(jnp.bfloat16)


def mlp_in(clips, order, ids, modulation, parts, w_in):
    rows = parts[0].shape[0]
    width, units = w_in.shape
    block = math.gcd(units, 512)
    return pl.pallas_call(
        functools.partial(mlp_in_kernel, clips, len(parts)),
        grid=(units // block,),
        out_shape=jax.ShapeDtypeStruct((rows, units), jnp.bfloat16),
        in_specs=[SMEM, VMEM, VMEM]
        + [VMEM] * len(parts)
        + [pl.BlockSpec((width, block), lambda i: (0, i))],
        out_specs=pl.BlockSpec((rows, block), lambda i: (0, i)),
        scratch_shapes=[pltpu.VMEM((rows, width), jnp.bfloat16)],
        compiler_params=params(MLP_GRANT),
        cost_estimate=cost(2 * rows * width * units, 2 * width * units),
        name="mlp_in",
    )(order, ids[:, None], modulation, *parts, w_in)


def mlp_out_kernel(hidden, w_out, branch):
    branch[...] = jnp.dot(hidden[...], w_out[...], preferred_element_type=jnp.float32)


def mlp_out(hidden, w_out):
    rows, units = hidden.shape
    width = w_out.shape[1]
    block = math.gcd(width, 512)
    return pl.pallas_call(
        mlp_out_kernel,
        grid=(width // block,),
        out_shape=jax.ShapeDtypeStruct((rows, width), jnp.float32),
        in_specs=[VMEM, pl.BlockSpec((units, block), lambda i: (0, i))],
        out_specs=pl.BlockSpec((rows, block), lambda i: (0, i)),
        compiler_params=params(MLP_GRANT),
        cost_estimate=cost(2 * rows * width * units, 2 * width * units + 4 * rows * width),
        name="mlp_out",
    )(hidden, w_out)


def project_kernel(ways, first, side, blocks, place, *refs):
    pieces = 2 * ways
    attended = refs[:ways]
    got, w_hbm, mlp_hbm, out, gathered, w, branch, sems = refs[ways:]
    half, width = out.shape
    share = mlp_hbm.shape[0] // 2
    block = width // blocks
    owner = lax.bitwise_xor(place[2], side)
    start = pl.multiple_of(owner * share + first, math.gcd(share, half))
    rows = pltpu.make_async_copy(mlp_hbm.at[pl.ds(start, half)], branch, sems.at[blocks])
    copies = []
    for i in range(blocks):
        columns = slice(i * block, (i + 1) * block)
        copies.append(pltpu.make_async_copy(w_hbm.at[:, columns], w.at[:, columns], sems.at[i]))
    for copy in [copies[0], rows] + copies[1:]:
        copy.start()
    at = pl.multiple_of(owner * half, half)
    for i in range(pieces):
        head = met(place, i % ways, i // ways)
        columns = pl.ds(pl.multiple_of(head * HD, HD), HD)
        if i < ways:
            gathered[:, columns] = attended[i][0, pl.ds(at, half), :]
        else:
            gathered[:, columns] = got[i - ways, pl.ds(at, half), :]
    for i in range(blocks):
        columns = slice(i * block, (i + 1) * block)
        copies[i].wait()
        product = jnp.dot(gathered[...], w[:, columns], preferred_element_type=jnp.float32)
        if i == 0:
            rows.wait()
        out[:, columns] = (branch[:, columns] + product).astype(out.dtype)


def project(scalars, attended, got, w_attn_out, mlp_branch, first, side, dtype, name):
    width = mlp_branch.shape[1]
    ways, half = len(attended), got.shape[1] // 2
    inputs = w_attn_out.shape[0]
    blocks = width // math.gcd(width, 768)
    return pl.pallas_call(
        functools.partial(project_kernel, ways, first, side, blocks),
        out_shape=jax.ShapeDtypeStruct((half, width), dtype),
        in_specs=[SMEM] + [VMEM] * (ways + 1) + [HBM, HBM],
        out_specs=VMEM,
        scratch_shapes=[
            pltpu.VMEM((half, inputs), jnp.bfloat16),
            pltpu.VMEM((inputs, width), jnp.bfloat16),
            pltpu.VMEM((half, width), jnp.float32),
            pltpu.SemaphoreType.DMA((blocks + 1,)),
        ],
        compiler_params=params(PROJECT_GRANT),
        cost_estimate=cost(1, 1),
        name=name,
    )(scalars, *attended, got, w_attn_out, mlp_branch)


def per_device(
    tokens,
    queries,
    key_rows,
    value_rows,
    clip_ids,
    causal,
    modulation,
    w_mlp,
    w_attn_out,
    w_mlp_out,
):
    local_rows = queries.shape[0]
    heads = queries.shape[1] // HD
    clips = causal.shape[0]
    tp_size = lax.axis_size("tp")
    ctx_size = lax.axis_size("ctx")
    here = lax.axis_index("ctx")
    tp_here = lax.axis_index("tp")
    first_row = here * local_rows
    own_ids = lax.dynamic_slice_in_dim(clip_ids, first_row, local_rows)
    clip_starts = jnp.sum(
        (clip_ids[None, :] < jnp.arange(clips + 1, dtype=jnp.int32)[:, None]).astype(jnp.int32),
        axis=1,
    )
    clip_scalars = jnp.concatenate([clip_starts, causal])
    share = local_rows // tp_size

    chips = ctx_size // 2
    split = (
        tp_size == 2
        and ctx_size % 2 == 0
        and chips & (chips - 1) == 0
        and heads == chips
        and local_rows == 3 * LANES
    )
    if split:
        return exchanged(
            tokens, queries, key_rows, value_rows, own_ids, clip_scalars, clips, modulation,
            w_mlp, w_attn_out, w_mlp_out, chips,
        )

    place = jnp.stack([first_row, 0, tp_here])
    full_rows = lax.all_gather(tokens, "tp", axis=1, tiled=True)
    hidden = mlp_in(clips, place, own_ids, modulation, [full_rows], w_mlp)
    branch = mlp_out(hidden, w_mlp_out)
    all_keys = lax.all_gather(key_rows, "ctx", axis=0, tiled=True)
    all_values = lax.all_gather(value_rows, "ctx", axis=0, tiled=True)
    attended = []
    for head in range(heads):
        columns = slice(head * HD, (head + 1) * HD)
        kv = jnp.stack([all_keys[:, columns], value_blocks(all_values[:, columns])])
        k, v = assemble(clips, clip_scalars, place, [kv[:, None]], False)
        attended.extend(
            attention(
                clips, clip_scalars, place, [queries[None, None, :, columns]], 0, local_rows,
                k, v, local_rows // 2, None, "attention",
            )
        )
    branch = lax.psum_scatter(
        branch
        + jnp.dot(jnp.concatenate([one[0] for one in attended], axis=1), w_attn_out, preferred_element_type=jnp.float32),
        "tp",
        scatter_dimension=0,
        tiled=True,
    )
    residual = lax.dynamic_slice_in_dim(full_rows, tp_here * share, share, 0)
    share_ids = lax.dynamic_slice_in_dim(own_ids, tp_here * share, share)
    gate_rows = select_rows(share_ids[:, None], modulation[2], clips)
    return residual.astype(jnp.float32) + gate_rows * branch


def exchanged(
    tokens, queries, key_rows, value_rows, own_ids, clip_scalars, clips, modulation,
    w_mlp, w_attn_out, w_mlp_out, chips,
):
    local_rows = queries.shape[0]
    share = local_rows // 2
    here = lax.axis_index("ctx")
    tp_here = lax.axis_index("tp")
    ways = chips // 2
    chunk_rows = (2 * LANES, LANES)

    def swap_tp(array):
        return lax.ppermute(array, "tp", [(0, 1), (1, 0)])

    def swap_cores(array):
        pairs = [(2 * i + c, 2 * i + 1 - c) for i in range(chips) for c in (0, 1)]
        return lax.ppermute(array, "ctx", pairs)

    def exchange(array, m):
        pairs = [(2 * i + c, 2 * (i ^ (2 * m + c)) + c) for i in range(chips) for c in (0, 1)]
        return lax.ppermute(array, "ctx", pairs)

    place = jnp.stack([here // 2, here % 2, tp_here])
    other_half = swap_tp(tokens)
    keep, give = split_heads(
        place, ways, chunk_rows, queries, key_rows, value_rows
    )
    messages = pack(keep, swap_cores(give))
    own_pieces = [None] * ways
    for m in reversed(range(ways)):
        own_pieces[m] = exchange(messages[m], m)
    parts = [tokens, other_half]
    hidden = mlp_in(clips, place, own_ids, modulation, parts, w_mlp)
    mlp_branch = mlp_out(hidden, w_mlp_out)
    for m in reversed(range(ways)):
        own_pieces[m], mlp_branch = lax.optimization_barrier((own_pieces[m], mlp_branch))
    core_pieces = [swap_cores(piece) for piece in own_pieces]

    k, v = assemble(clips, clip_scalars, place, own_pieces + core_pieces, True)

    def attend(chunk, some, clip_scalars, name):
        start = sum(chunk_rows[:chunk])
        return attention(
            clips, clip_scalars, place, [own_pieces[m] for m in some], start,
            chunk_rows[chunk], k, v, share, some[0], name,
        )

    def send_back(outs, some):
        return [exchange(piece, m) for m, piece in zip(some, outs)]

    def kept_rows(chunk, attended, got):
        return project(
            place, attended, got, w_attn_out, mlp_branch,
            sum(chunk_rows[:chunk]) // 2, 0, jnp.float32, "project_kept_%d" % chunk,
        )

    def sent_rows(chunk, attended, got):
        return project(
            place, attended, got, w_attn_out, mlp_branch,
            sum(chunk_rows[:chunk]) // 2, 1, jnp.bfloat16, "project_sent_%d" % chunk,
        )

    near, far = range(ways // 2), range(ways // 2, ways)
    first_outs = attend(0, range(ways), clip_scalars, "attention_0")
    first = send_back(first_outs, range(ways))
    clip_scalars, _ = lax.optimization_barrier((clip_scalars, first_outs[0]))
    far_outs = attend(1, far, clip_scalars, "attention_1_far")
    first, far_outs = lax.optimization_barrier((first, far_outs))
    first_got = swap_cores(pick_others(first))
    first_sent = sent_rows(0, first, first_got)
    far_second = send_back(far_outs, far)
    clip_scalars, first_sent = lax.optimization_barrier((clip_scalars, first_sent))
    first_came = swap_tp(first_sent)
    near_outs = attend(1, near, clip_scalars, "attention_1_near")
    far_second, near_outs = lax.optimization_barrier((far_second, near_outs))
    second = send_back(near_outs, near) + far_second
    first, near_outs = lax.optimization_barrier((first, near_outs))
    first_kept = kept_rows(0, first, first_got)
    second, first_kept = lax.optimization_barrier((second, first_kept))
    second_got = swap_cores(pick_others(second))
    second_sent = sent_rows(1, second, second_got)
    second_sent, first_came = lax.optimization_barrier((second_sent, first_came))
    second_came = swap_tp(second_sent)
    tokens, other_half, own_ids, second, second_sent = lax.optimization_barrier(
        (tokens, other_half, own_ids, second, second_sent)
    )
    second_kept = kept_rows(1, second, second_got)
    own = [
        lax.dynamic_slice_in_dim(part, tp_here * share, share, 0) for part in (tokens, other_half)
    ]
    residual = jnp.where(
        tp_here == 0, jnp.concatenate(own, axis=1), jnp.concatenate(own[::-1], axis=1)
    ).astype(jnp.float32)
    share_ids = lax.dynamic_slice_in_dim(own_ids, tp_here * share, share)
    gate_rows = select_rows(share_ids[:, None], modulation[2], clips)
    cut = first_kept.shape[0]
    begun = residual[:cut] + gate_rows[:cut] * (first_kept + first_came.astype(jnp.float32))
    rest = residual[cut:] + gate_rows[cut:] * second_kept
    begun, rest, gate_rest = lax.optimization_barrier((begun, rest, gate_rows[cut:]))
    rest = rest + gate_rest * second_came.astype(jnp.float32)
    return jnp.concatenate([begun, rest], axis=0)


def solution(mesh):
    in_specs = (
        P("ctx", "tp"),
        P("ctx", "tp"),
        P("ctx", "tp"),
        P("ctx", "tp"),
        P(),
        P(),
        P(),
        P(None, "tp"),
        P("tp", None),
        P("tp", None),
    )
    out_specs = P(("ctx", "tp"), None)
    return jax.shard_map(
        per_device, mesh=mesh, in_specs=in_specs, out_specs=out_specs, check_vma=False
    )
```

```python
import functools
import math

import jax
import jax.numpy as jnp
from jax import lax
from jax.experimental import pallas as pl
from jax.experimental.pallas import tpu as pltpu
from jax.sharding import PartitionSpec as P

HD = 128
LANES = 128
ONES_ROWS = 16
KEY_WIDTH = 2 * HD
MASKED = -3e38
COST_SCALE = 1
SPLIT_GRANT = 60
MLP_GRANT = 44
PROJECT_GRANT = 50
START_MAX = -1e30
EPS_NORM = 1e-06
EXP2_SCALE = math.log2(math.e) / math.sqrt(HD)

ANY = pl.BlockSpec(memory_space=pl.ANY)
HBM = pl.BlockSpec(memory_space=pltpu.HBM)
SMEM = pl.BlockSpec(memory_space=pltpu.SMEM)
VMEM = pl.BlockSpec(memory_space=pltpu.VMEM)


def params(mebibytes):
    return pltpu.CompilerParams(vmem_limit_bytes=mebibytes << 20)


def cost(flops, nbytes, exps=0):
    return pl.CostEstimate(
        flops=flops // COST_SCALE, bytes_accessed=nbytes // COST_SCALE, transcendentals=exps // COST_SCALE
    )


def met(place, m, other):
    core = lax.bitwise_xor(place[1], other)
    return lax.bitwise_xor(place[0], 2 * m + core)


def token_base(place, m, other, group, rows):
    core = lax.bitwise_xor(lax.bitwise_xor(place[1], other), group)
    return (met(place, m, other) * 2 + core) * rows


def split_kernel(
    ways, chunk_rows, place, q_hbm, k_hbm, v_hbm, keep, give, q, k, v, sems
):
    rows = q.shape[0]
    share = rows // 2
    copies = [
        pltpu.make_async_copy(source, target, sems.at[i])
        for i, (source, target) in enumerate(((k_hbm, k), (v_hbm, v), (q_hbm, q)))
    ]
    for copy in copies:
        copy.start()
    for copy in copies:
        copy.wait()
    for side, out in enumerate((give, keep)):
        for m in range(ways):
            head = met(place, m, 1 - side)
            columns = pl.ds(pl.multiple_of(head * HD, HD), HD)
            out[m, 0] = k[:, columns]
            for at in range(0, rows, LANES):
                block = v[at : at + LANES, columns].astype(jnp.float32)
                out[m, 1, at : at + LANES, :] = jnp.transpose(block).astype(jnp.bfloat16)
            first = 0
            for count in chunk_rows:
                half = count // 2
                start = 2 * first
                out[m, 2, start : start + half] = q[first : first + half, columns]
                out[m, 2, start + half : start + count] = q[
                    share + first : share + first + half, columns
                ]
                first += half


def split_heads(scalars, ways, chunk_rows, queries, key_rows, value_rows):
    rows = queries.shape[0]
    shape = jax.ShapeDtypeStruct((ways, 3, rows, HD), jnp.bfloat16)
    return pl.pallas_call(
        functools.partial(split_kernel, ways, chunk_rows),
        out_shape=[shape, shape],
        in_specs=[SMEM, HBM, HBM, HBM],
        out_specs=[VMEM, VMEM],
        scratch_shapes=[pltpu.VMEM(queries.shape, jnp.bfloat16)] * 3
        + [pltpu.SemaphoreType.DMA((3,))],
        compiler_params=params(SPLIT_GRANT),
        name="split_heads",
    )(scalars, queries, key_rows, value_rows)


def pack_kernel(ways, keep, got, *refs):
    outs, sems = refs[:ways], refs[ways]
    copies = []
    for m in reversed(range(ways)):
        for i, source in enumerate((keep, got)):
            copies.append(
                pltpu.make_async_copy(source.at[m], outs[m].at[:, i], sems.at[2 * m + i])
            )
            copies[-1].start()
    for copy in copies:
        copy.wait()


def pack(keep, got):
    ways, arrays, rows, _ = keep.shape
    return pl.pallas_call(
        functools.partial(pack_kernel, ways),
        out_shape=[jax.ShapeDtypeStruct((arrays, 2, rows, HD), jnp.bfloat16)] * ways,
        in_specs=[ANY, ANY],
        out_specs=[ANY] * ways,
        scratch_shapes=[pltpu.SemaphoreType.DMA((2 * ways,))],
        compiler_params=params(4),
        name="pack",
    )(keep, got)


def pick_kernel(ways, *refs):
    pieces, out, sems = refs[:ways], refs[ways], refs[ways + 1]
    copies = []
    for m in range(ways):
        copies.append(pltpu.make_async_copy(pieces[m].at[1], out.at[m], sems.at[m]))
        copies[-1].start()
    for copy in copies:
        copy.wait()


def pick_others(pieces):
    _, rows, width = pieces[0].shape
    return pl.pallas_call(
        functools.partial(pick_kernel, len(pieces)),
        out_shape=jax.ShapeDtypeStruct((len(pieces), rows, width), jnp.bfloat16),
        in_specs=[ANY] * len(pieces),
        out_specs=ANY,
        scratch_shapes=[pltpu.SemaphoreType.DMA((len(pieces),))],
        compiler_params=params(4),
        name="pick_others",
    )(*pieces)


def clip_lanes(scalars, clips):
    lane = lax.broadcasted_iota(jnp.int32, (1, HD), 1)
    low = jnp.zeros_like(lane)
    high = jnp.zeros_like(lane)
    for clip in range(clips):
        low = jnp.where(lane == clip, scalars[clip], low)
        high = jnp.where(lane == clip, scalars[clip + 1], high)
    return low, high


def assemble_kernel(clips, n_kv, exchanged_pieces, scalars, place, *refs):
    pieces = refs[:n_kv]
    k, v, sems = refs[n_kv:]
    all_keys = k.shape[0]
    copies = []

    def load(source, target):
        copies.append(pltpu.make_async_copy(source, target, sems.at[len(copies)]))
        copies[-1].start()

    for i, piece in enumerate(pieces):
        groups, count = piece.shape[1:3]
        for group in range(groups):
            base = 0
            if exchanged_pieces:
                ways = n_kv // 2
                base = token_base(place, i % ways, i // ways, group, count)
                base = pl.multiple_of(base, LANES)
            load(piece.at[0, group], k.at[pl.ds(base, count), 0:HD])
            for at in range(0, count, LANES):
                columns = pl.ds(pl.multiple_of(base + at, LANES), LANES)
                load(piece.at[1, group, at : at + LANES], v.at[0:HD, columns])
    low, high = clip_lanes(scalars, clips)
    step = math.gcd(all_keys, 768)
    for at in range(0, all_keys, step):
        pos = at + lax.broadcasted_iota(jnp.int32, (step, HD), 0)
        inside = (pos >= low) & (pos < high)
        k[at : at + step, HD:] = jnp.where(inside, 1.0, 0.0).astype(jnp.bfloat16)
    v[HD:, :] = jnp.ones((v.shape[0] - HD, all_keys), jnp.bfloat16)
    for copy in copies:
        copy.wait()


def assemble(clips, scalars, place, kv_pieces, exchanged_pieces):
    all_keys = sum(piece.shape[1] * piece.shape[2] for piece in kv_pieces)
    n_sems = sum(piece.shape[1] * (1 + piece.shape[2] // LANES) for piece in kv_pieces)
    return pl.pallas_call(
        functools.partial(assemble_kernel, clips, len(kv_pieces), exchanged_pieces),
        out_shape=[
            jax.ShapeDtypeStruct((all_keys, KEY_WIDTH), jnp.bfloat16),
            jax.ShapeDtypeStruct((HD + ONES_ROWS, all_keys), jnp.bfloat16),
        ],
        in_specs=[SMEM, SMEM] + [ANY] * len(kv_pieces),
        out_specs=[VMEM, VMEM],
        scratch_shapes=[pltpu.SemaphoreType.DMA((n_sems,))],
        compiler_params=params(16),
        name="assemble",
    )(scalars, place, *kv_pieces)


def span_of(scalars, clips, pos):
    low = jnp.zeros_like(pos)
    high = jnp.zeros_like(pos)
    for clip in range(clips):
        inside = pos >= scalars[clip]
        end = jnp.where(scalars[clips + 1 + clip] != 0, pos + 1, scalars[clip + 1])
        low = jnp.where(inside, scalars[clip], low)
        high = jnp.where(inside, end, high)
    return low, high


def attention_kernel(
    clips, share, start, key_tile, first_way, scalars, place, k, v, *refs
):
    n_query = (len(refs) - 8) // 2
    query_hbm = refs[:n_query]
    out_hbm = refs[n_query : 2 * n_query]
    q, out, total, peak, score_a, score_b, block_peak, sems = refs[2 * n_query :]
    width = q.shape[1]
    groups, rows, _ = out_hbm[0].shape
    half = rows // 2
    none_causal = 1 << 30
    copies = []
    for i in range(n_query):
        arrays = query_hbm[i].shape[0]
        for group in range(groups):
            copies.append(
                pltpu.make_async_copy(
                    query_hbm[i].at[arrays - 1, group, start : start + rows],
                    q.at[i, group * rows : (group + 1) * rows, 0:HD],
                    sems.at[i * groups + group],
                )
            )
            copies[-1].start()
    clip_low, clip_high = clip_lanes(scalars, clips)
    for copy in copies:
        copy.wait()
    scores = [score_a, score_b]
    leaving = [
        [
            pltpu.make_async_copy(
                out.at[i, group * rows : (group + 1) * rows],
                out_hbm[i].at[group],
                sems.at[i * groups + group],
            )
            for group in range(groups)
        ]
        for i in range(n_query)
    ]

    def positions(shape, axis, firsts):
        index = lax.broadcasted_iota(jnp.int32, shape, axis)
        pos = index
        for group, first in enumerate(firsts):
            at = group * rows
            pos = jnp.where(index >= at, index + (first - at), pos)
            pos = jnp.where(index >= at + half, index + (first + share - at - half), pos)
        return pos

    def one_tile(piece, _):
        if first_way is not None:
            firsts = [
                token_base(place, first_way + piece, 0, group, 2 * share) + start // 2
                for group in range(groups)
            ]
        else:
            firsts = [place[0]]
        begin, end, causal_from = none_causal, 0, none_causal
        for first in firsts:
            last = first + share + half - 1
            begin = jnp.minimum(begin, span_of(scalars, clips, first)[0])
            end = jnp.maximum(end, span_of(scalars, clips, last)[1])
            for clip in range(clips):
                met = (first < scalars[clip + 1]) & (last >= scalars[clip])
                met = met & (scalars[clips + 1 + clip] != 0)
                causal_from = jnp.where(
                    met, jnp.minimum(causal_from, jnp.maximum(first, scalars[clip])), causal_from
                )
        begin = begin // key_tile
        end = (end + key_tile - 1) // key_tile
        pos = positions((1, width), 1, firsts)
        last_key = jnp.full_like(pos, none_causal)
        for clip in range(clips):
            inside = (pos >= scalars[clip]) & (pos < scalars[clip + 1])
            inside = inside & (scalars[clips + 1 + clip] != 0)
            last_key = jnp.where(inside, pos, last_key)
        row_pos = positions((width, HD), 0, firsts)
        inside = (row_pos >= clip_low) & (row_pos < clip_high)
        q[piece, :, HD:] = jnp.where(inside, 0.0, MASKED).astype(jnp.bfloat16)
        total[...] = jnp.zeros_like(total)
        peak[...] = jnp.full_like(peak, START_MAX)

        def multiply(tile, slot):
            keys = k[pl.ds(pl.multiple_of(tile * key_tile, key_tile), key_tile), :]
            block = lax.dot_general(
                keys, q[piece], (((1,), (1,)), ((), ())), preferred_element_type=jnp.float32
            )
            scores[slot][...] = block
            block_peak[slot] = jnp.max(block, axis=0, keepdims=True)

        def mask(tile, slot):
            @pl.when((tile + 1) * key_tile - 1 > causal_from)
            def _():
                key_pos = tile * key_tile + lax.broadcasted_iota(jnp.int32, (key_tile, 1), 0)
                block = jnp.where(key_pos <= last_key, scores[slot][...], MASKED)
                scores[slot][...] = block
                block_peak[slot] = jnp.max(block, axis=0, keepdims=True)

        def gather(tile, slot):
            old = peak[...]
            new = jnp.maximum(old, block_peak[slot])
            peak[...] = new
            factor = jnp.exp2((old - new) * EXP2_SCALE)
            weights = jnp.exp2(scores[slot][...] * EXP2_SCALE - new * EXP2_SCALE)
            values = v[:, pl.ds(pl.multiple_of(tile * key_tile, key_tile), key_tile)]
            total[...] = total[...] * factor + jnp.dot(
                values, weights.astype(jnp.bfloat16), preferred_element_type=jnp.float32
            )

        multiply(begin, 0)
        mask(begin, 0)
        count = end - begin

        def two_tiles(pair, _):
            tile = begin + 2 * pair
            multiply(tile + 1, 1)
            gather(tile, 0)
            mask(tile + 1, 1)
            later = jnp.minimum(tile + 2, end - 1)
            multiply(later, 0)
            gather(tile + 1, 1)
            mask(later, 0)
            return 0

        lax.fori_loop(0, count // 2, two_tiles, 0)

        @pl.when(count % 2 == 1)
        def _():
            gather(end - 1, 0)

        both = total[...]
        out[piece] = jnp.transpose(both[:HD] / both[HD : HD + 1]).astype(jnp.bfloat16)
        return 0

    def tile_and_leave(piece, _):
        one_tile(piece, _)
        for i in range(n_query):

            @pl.when(piece == i)
            def _():
                for copy in leaving[i]:
                    copy.start()

        return 0

    lax.fori_loop(0, n_query, tile_and_leave, 0)
    for some in leaving:
        for copy in some:
            copy.wait()


def attention(
    clips, scalars, place, queries, start, rows, k, v, share, first_way, name
):
    n_query = len(queries)
    groups = queries[0].shape[1]
    width = groups * rows
    all_keys = k.shape[0]
    key_tile = math.gcd(all_keys, 768)
    return pl.pallas_call(
        functools.partial(
            attention_kernel, clips, share, start, key_tile, first_way
        ),
        out_shape=[jax.ShapeDtypeStruct((groups, rows, HD), jnp.bfloat16)] * n_query,
        in_specs=[SMEM, SMEM, VMEM, VMEM] + [ANY] * n_query,
        out_specs=[ANY] * n_query,
        scratch_shapes=[
            pltpu.VMEM((n_query, width, KEY_WIDTH), jnp.bfloat16),
            pltpu.VMEM((n_query, width, HD), jnp.bfloat16),
            pltpu.VMEM((HD + ONES_ROWS, width), jnp.float32),
            pltpu.VMEM((1, width), jnp.float32),
            pltpu.VMEM((key_tile, width), jnp.float32),
            pltpu.VMEM((key_tile, width), jnp.float32),
            pltpu.VMEM((2, 1, width), jnp.float32),
            pltpu.SemaphoreType.DMA((n_query * groups,)),
        ],
        compiler_params=params(20),
        cost_estimate=cost(
            4 * n_query * width * all_keys * HD, 4 * all_keys * HD, n_query * width * all_keys
        ),
        name=name,
    )(scalars, place, k, v, *queries)


def value_blocks(values):
    count = values.shape[0]
    return jnp.swapaxes(values.reshape(count // LANES, LANES, HD), 1, 2).reshape(count, HD)


def select_rows(ids, table, clips):
    picked = jnp.broadcast_to(table[0:1], (ids.shape[0], table.shape[1]))
    for clip in range(1, clips):
        picked = jnp.where(ids == clip, table[clip : clip + 1], picked)
    return picked


def mlp_in_kernel(clips, n_parts, place, ids_ref, modulation_ref, *refs):
    parts = refs[:n_parts]
    w_in, hidden, modulated = refs[n_parts:]
    width = modulated.shape[1]

    @pl.when(pl.program_id(0) == 0)
    def _():
        part_width = width // n_parts
        mean = sum(
            jnp.sum(part[...].astype(jnp.float32), axis=1, keepdims=True) for part in parts
        ) / width
        variance = sum(
            jnp.sum((part[...].astype(jnp.float32) - mean) ** 2, axis=1, keepdims=True)
            for part in parts
        ) / width
        inverse = lax.rsqrt(variance + EPS_NORM)
        ids = ids_ref[...]
        for i, part in enumerate(parts):
            part_at = lax.bitwise_xor(place[2], i) if n_parts > 1 else 0
            columns = pl.ds(pl.multiple_of(part_at * part_width, LANES), part_width)
            normed = (part[...].astype(jnp.float32) - mean) * inverse
            shift = select_rows(ids, modulation_ref[0, :, columns], clips)
            scale = select_rows(ids, modulation_ref[1, :, columns], clips)
            modulated[:, columns] = (normed * (1.0 + scale) + shift).astype(jnp.bfloat16)

    hidden[...] = jax.nn.gelu(
        jnp.dot(modulated[...], w_in[...], preferred_element_type=jnp.float32), approximate=True
    ).astype(jnp.bfloat16)


def mlp_in(clips, order, ids, modulation, parts, w_in):
    rows = parts[0].shape[0]
    width, units = w_in.shape
    block = math.gcd(units, 512)
    return pl.pallas_call(
        functools.partial(mlp_in_kernel, clips, len(parts)),
        grid=(units // block,),
        out_shape=jax.ShapeDtypeStruct((rows, units), jnp.bfloat16),
        in_specs=[SMEM, VMEM, VMEM]
        + [VMEM] * len(parts)
        + [pl.BlockSpec((width, block), lambda i: (0, i))],
        out_specs=pl.BlockSpec((rows, block), lambda i: (0, i)),
        scratch_shapes=[pltpu.VMEM((rows, width), jnp.bfloat16)],
        compiler_params=params(MLP_GRANT),
        cost_estimate=cost(2 * rows * width * units, 2 * width * units),
        name="mlp_in",
    )(order, ids[:, None], modulation, *parts, w_in)


def mlp_out_kernel(hidden, w_out, branch):
    branch[...] = jnp.dot(hidden[...], w_out[...], preferred_element_type=jnp.float32)


def mlp_out(hidden, w_out):
    rows, units = hidden.shape
    width = w_out.shape[1]
    block = math.gcd(width, 512)
    return pl.pallas_call(
        mlp_out_kernel,
        grid=(width // block,),
        out_shape=jax.ShapeDtypeStruct((rows, width), jnp.float32),
        in_specs=[VMEM, pl.BlockSpec((units, block), lambda i: (0, i))],
        out_specs=pl.BlockSpec((rows, block), lambda i: (0, i)),
        compiler_params=params(MLP_GRANT),
        cost_estimate=cost(2 * rows * width * units, 2 * width * units + 4 * rows * width),
        name="mlp_out",
    )(hidden, w_out)


def project_kernel(ways, first, side, blocks, place, *refs):
    pieces = 2 * ways
    attended = refs[:ways]
    got, w_hbm, mlp_hbm, out, gathered, w, branch, sems = refs[ways:]
    half, width = out.shape
    share = mlp_hbm.shape[0] // 2
    block = width // blocks
    owner = lax.bitwise_xor(place[2], side)
    start = pl.multiple_of(owner * share + first, math.gcd(share, half))
    rows = pltpu.make_async_copy(mlp_hbm.at[pl.ds(start, half)], branch, sems.at[blocks])
    copies = []
    for i in range(blocks):
        columns = slice(i * block, (i + 1) * block)
        copies.append(pltpu.make_async_copy(w_hbm.at[:, columns], w.at[:, columns], sems.at[i]))
    for copy in [copies[0], rows] + copies[1:]:
        copy.start()
    at = pl.multiple_of(owner * half, half)
    for i in range(pieces):
        head = met(place, i % ways, i // ways)
        columns = pl.ds(pl.multiple_of(head * HD, HD), HD)
        if i < ways:
            gathered[:, columns] = attended[i][0, pl.ds(at, half), :]
        else:
            gathered[:, columns] = got[i - ways, pl.ds(at, half), :]
    for i in range(blocks):
        columns = slice(i * block, (i + 1) * block)
        copies[i].wait()
        product = jnp.dot(gathered[...], w[:, columns], preferred_element_type=jnp.float32)
        if i == 0:
            rows.wait()
        out[:, columns] = (branch[:, columns] + product).astype(out.dtype)


def project(scalars, attended, got, w_attn_out, mlp_branch, first, side, dtype, name):
    width = mlp_branch.shape[1]
    ways, half = len(attended), got.shape[1] // 2
    inputs = w_attn_out.shape[0]
    blocks = width // math.gcd(width, 768)
    return pl.pallas_call(
        functools.partial(project_kernel, ways, first, side, blocks),
        out_shape=jax.ShapeDtypeStruct((half, width), dtype),
        in_specs=[SMEM] + [VMEM] * (ways + 1) + [HBM, HBM],
        out_specs=VMEM,
        scratch_shapes=[
            pltpu.VMEM((half, inputs), jnp.bfloat16),
            pltpu.VMEM((inputs, width), jnp.bfloat16),
            pltpu.VMEM((half, width), jnp.float32),
            pltpu.SemaphoreType.DMA((blocks + 1,)),
        ],
        compiler_params=params(PROJECT_GRANT),
        cost_estimate=cost(1, 1),
        name=name,
    )(scalars, *attended, got, w_attn_out, mlp_branch)


def per_device(
    tokens,
    queries,
    key_rows,
    value_rows,
    clip_ids,
    causal,
    modulation,
    w_mlp,
    w_attn_out,
    w_mlp_out,
):
    local_rows = queries.shape[0]
    heads = queries.shape[1] // HD
    clips = causal.shape[0]
    tp_size = lax.axis_size("tp")
    ctx_size = lax.axis_size("ctx")
    here = lax.axis_index("ctx")
    tp_here = lax.axis_index("tp")
    first_row = here * local_rows
    own_ids = lax.dynamic_slice_in_dim(clip_ids, first_row, local_rows)
    clip_starts = jnp.sum(
        (clip_ids[None, :] < jnp.arange(clips + 1, dtype=jnp.int32)[:, None]).astype(jnp.int32),
        axis=1,
    )
    clip_scalars = jnp.concatenate([clip_starts, causal])
    share = local_rows // tp_size

    chips = ctx_size // 2
    split = (
        tp_size == 2
        and ctx_size % 2 == 0
        and chips & (chips - 1) == 0
        and heads == chips
        and local_rows == 3 * LANES
    )
    if split:
        return exchanged(
            tokens, queries, key_rows, value_rows, own_ids, clip_scalars, clips, modulation,
            w_mlp, w_attn_out, w_mlp_out, chips,
        )

    place = jnp.stack([first_row, 0, tp_here])
    full_rows = lax.all_gather(tokens, "tp", axis=1, tiled=True)
    hidden = mlp_in(clips, place, own_ids, modulation, [full_rows], w_mlp)
    branch = mlp_out(hidden, w_mlp_out)
    all_keys = lax.all_gather(key_rows, "ctx", axis=0, tiled=True)
    all_values = lax.all_gather(value_rows, "ctx", axis=0, tiled=True)
    attended = []
    for head in range(heads):
        columns = slice(head * HD, (head + 1) * HD)
        kv = jnp.stack([all_keys[:, columns], value_blocks(all_values[:, columns])])
        k, v = assemble(clips, clip_scalars, place, [kv[:, None]], False)
        attended.extend(
            attention(
                clips, clip_scalars, place, [queries[None, None, :, columns]], 0, local_rows,
                k, v, local_rows // 2, None, "attention",
            )
        )
    branch = lax.psum_scatter(
        branch
        + jnp.dot(jnp.concatenate([one[0] for one in attended], axis=1), w_attn_out, preferred_element_type=jnp.float32),
        "tp",
        scatter_dimension=0,
        tiled=True,
    )
    residual = lax.dynamic_slice_in_dim(full_rows, tp_here * share, share, 0)
    share_ids = lax.dynamic_slice_in_dim(own_ids, tp_here * share, share)
    gate_rows = select_rows(share_ids[:, None], modulation[2], clips)
    return residual.astype(jnp.float32) + gate_rows * branch


def exchanged(
    tokens, queries, key_rows, value_rows, own_ids, clip_scalars, clips, modulation,
    w_mlp, w_attn_out, w_mlp_out, chips,
):
    local_rows = queries.shape[0]
    share = local_rows // 2
    here = lax.axis_index("ctx")
    tp_here = lax.axis_index("tp")
    ways = chips // 2
    chunk_rows = (2 * LANES, LANES)

    def swap_tp(array):
        return lax.ppermute(array, "tp", [(0, 1), (1, 0)])

    def swap_cores(array):
        pairs = [(2 * i + c, 2 * i + 1 - c) for i in range(chips) for c in (0, 1)]
        return lax.ppermute(array, "ctx", pairs)

    def exchange(array, m):
        pairs = [(2 * i + c, 2 * (i ^ (2 * m + c)) + c) for i in range(chips) for c in (0, 1)]
        return lax.ppermute(array, "ctx", pairs)

    place = jnp.stack([here // 2, here % 2, tp_here])
    other_half = swap_tp(tokens)
    keep, give = split_heads(
        place, ways, chunk_rows, queries, key_rows, value_rows
    )
    messages = pack(keep, swap_cores(give))
    own_pieces = [None] * ways
    for m in reversed(range(ways)):
        own_pieces[m] = exchange(messages[m], m)
    parts = [tokens, other_half]
    hidden = mlp_in(clips, place, own_ids, modulation, parts, w_mlp)
    mlp_branch = mlp_out(hidden, w_mlp_out)
    for m in reversed(range(ways)):
        own_pieces[m], mlp_branch = lax.optimization_barrier((own_pieces[m], mlp_branch))
    core_pieces = [swap_cores(piece) for piece in own_pieces]

    k, v = assemble(clips, clip_scalars, place, own_pieces + core_pieces, True)

    def attend(chunk, some, clip_scalars, name):
        start = sum(chunk_rows[:chunk])
        return attention(
            clips, clip_scalars, place, [own_pieces[m] for m in some], start,
            chunk_rows[chunk], k, v, share, some[0], name,
        )

    def send_back(outs, some):
        return [exchange(piece, m) for m, piece in zip(some, outs)]

    def kept_rows(chunk, attended, got):
        return project(
            place, attended, got, w_attn_out, mlp_branch,
            sum(chunk_rows[:chunk]) // 2, 0, jnp.float32, "project_kept_%d" % chunk,
        )

    def sent_rows(chunk, attended, got):
        return project(
            place, attended, got, w_attn_out, mlp_branch,
            sum(chunk_rows[:chunk]) // 2, 1, jnp.bfloat16, "project_sent_%d" % chunk,
        )

    near, far = range(ways // 2), range(ways // 2, ways)
    first_outs = attend(0, range(ways), clip_scalars, "attention_0")
    first = send_back(first_outs, range(ways))
    clip_scalars, _ = lax.optimization_barrier((clip_scalars, first_outs[0]))
    far_outs = attend(1, far, clip_scalars, "attention_1_far")
    first, far_outs = lax.optimization_barrier((first, far_outs))
    first_got = swap_cores(pick_others(first))
    first_sent = sent_rows(0, first, first_got)
    far_second = send_back(far_outs, far)
    clip_scalars, first_sent = lax.optimization_barrier((clip_scalars, first_sent))
    first_came = swap_tp(first_sent)
    near_outs = attend(1, near, clip_scalars, "attention_1_near")
    far_second, near_outs = lax.optimization_barrier((far_second, near_outs))
    second = send_back(near_outs, near) + far_second
    first, near_outs = lax.optimization_barrier((first, near_outs))
    first_kept = kept_rows(0, first, first_got)
    second, first_kept = lax.optimization_barrier((second, first_kept))
    second_got = swap_cores(pick_others(second))
    second_sent = sent_rows(1, second, second_got)
    second_sent, first_came = lax.optimization_barrier((second_sent, first_came))
    second_came = swap_tp(second_sent)
    tokens, other_half, own_ids, second, second_sent = lax.optimization_barrier(
        (tokens, other_half, own_ids, second, second_sent)
    )
    second_kept = kept_rows(1, second, second_got)
    own = [
        lax.dynamic_slice_in_dim(part, tp_here * share, share, 0) for part in (tokens, other_half)
    ]
    residual = jnp.where(
        tp_here == 0, jnp.concatenate(own, axis=1), jnp.concatenate(own[::-1], axis=1)
    ).astype(jnp.float32)
    share_ids = lax.dynamic_slice_in_dim(own_ids, tp_here * share, share)
    gate_rows = select_rows(share_ids[:, None], modulation[2], clips)
    cut = first_kept.shape[0]
    begun = residual[:cut] + gate_rows[:cut] * (first_kept + first_came.astype(jnp.float32))
    rest = residual[cut:] + gate_rows[cut:] * second_kept
    begun, rest, gate_rest = lax.optimization_barrier((begun, rest, gate_rows[cut:]))
    rest = rest + gate_rest * second_came.astype(jnp.float32)
    return jnp.concatenate([begun, rest], axis=0)


def solution(mesh):
    in_specs = (
        P("ctx", "tp"),
        P("ctx", "tp"),
        P("ctx", "tp"),
        P("ctx", "tp"),
        P(),
        P(),
        P(),
        P(None, "tp"),
        P("tp", None),
        P("tp", None),
    )
    out_specs = P(("ctx", "tp"), None)
    return jax.shard_map(
        per_device, mesh=mesh, in_specs=in_specs, out_specs=out_specs, check_vma=False
    )
```
